512 devices in a mesh: tok: 16 (over y, x), own: 32 (over z, core).
Axes of the slice: x: 4, y: 4, z: 16, core: 2. Of those that a mesh axis runs over, the one named last changes fastest.
Arguments:
- hidden: bfloat16 [2048, 24576], P('tok', 'own'), may hold values from -6 to 6
- grad_out: bfloat16 [2048, 6144], P('tok', 'own'), may hold values from -6 to 6
- old_weight: bfloat16 [768, 128, 128], P('own'), may hold values from -6 to 6
- old_first: bfloat16 [768, 128, 128], P('own'), may hold values from -1.5 to 1.5
- old_second: bfloat16 [768, 128, 128], P('own'), may hold values from 0.0049743652 to 0.19921875
- old_blocks: int32 [768, 2], replicated, may hold values from 0 to 191, as said below
- new_blocks: int32 [768, 2], replicated, may hold values from 0 to 191, as said below
- new_owner: int32 [768], replicated, may hold values from 0 to 31, as said below
Outputs:
- output: bfloat16 [2048, 6144], P('tok', 'own')
- new_weight: bfloat16 [768, 128, 128], P('own')
- new_first: bfloat16 [768, 128, 128], P('own')
- new_second: bfloat16 [768, 128, 128], P('own')
The draws below stay inside these ranges and needn't reach their ends.
Inputs may be any that keep to these rules, and one draw needn't show every extreme that they name: `old_blocks`: rows are (row block of the 24576 inputs, column block of the 6144 outputs); the old blocks are distinct, and each new entry is either the old block of that slot or a block found in neither list elsewhere. `new_blocks`: same form as old_blocks; the new blocks are distinct. Of the 24 blocks that one new owner receives, at most 1 has its row block among the 24576 / 32 input features held by any one device along own, and this bound of 1 is reached in every draw. `new_owner`: every owner receives exactly 24 blocks; the slots of one old owner send at most 1 block to one new owner, and 1 is reached in every draw.
All inputs are finite; a program needn't handle non-finite values.
Results may differ from the reference program's by a relative error of at most 0.022.
Values may be sent and summed in bfloat16 or wider, within the bound.
A program may use at most 64 MiB of HBM per device.

```python
import math
import jax
import jax.numpy as jnp
from jax import lax

D = 6144
FF = 24576
BLOCK = 128
TOK_GRP = 128
BLK_DEV = 24
NBLK = 768
TOKENS = 2048
N_TOK = 16
N_OWN = 32


def owner_targets(key):
    key = jax.random.fold_in(key, 5)
    offsets = jax.random.permutation(jax.random.fold_in(key, 1), N_OWN).astype(jnp.int32)
    shifts = offsets[jnp.arange(BLK_DEV, dtype=jnp.int32) % N_OWN]
    row_keys = jax.random.split(jax.random.fold_in(key, 2), N_OWN)
    orders = jax.vmap(lambda row_key: jax.random.permutation(row_key, BLK_DEV))(row_keys)
    relabel = jax.random.permutation(jax.random.fold_in(key, 3), N_OWN).astype(jnp.int32)
    sources = jnp.arange(N_OWN, dtype=jnp.int32)[:, None]
    targets = (sources + shifts[orders]) % N_OWN
    return relabel[targets].reshape(-1).astype(jnp.int32)


def block_lists(key):
    owner = owner_targets(key)
    key = jax.random.fold_in(key, 11)
    onehot = (owner[:, None] == jnp.arange(N_OWN, dtype=jnp.int32)[None, :]).astype(jnp.int32)
    before = jnp.cumsum(onehot, 0) - onehot
    rank = jnp.sum(before * onehot, 1).astype(jnp.int32)
    share_rows = FF // BLOCK // N_OWN
    col_count = D // BLOCK
    sigma = jax.random.permutation(jax.random.fold_in(key, 1), N_OWN).astype(jnp.int32)
    share = sigma[(owner + rank) % N_OWN]
    bases = jax.random.randint(jax.random.fold_in(key, 2), (N_OWN,), 0, col_count).astype(jnp.int32)
    column_order = jax.random.permutation(jax.random.fold_in(key, 3), col_count).astype(jnp.int32)
    new_col = column_order[(bases[share] + rank) % col_count]
    drop_col = column_order[(bases[share] + BLK_DEV + rank) % col_count]
    new_row = share * share_rows + jax.random.randint(jax.random.fold_in(key, 4), (NBLK,), 0, share_rows).astype(jnp.int32)
    drop_row = share * share_rows + jax.random.randint(jax.random.fold_in(key, 6), (NBLK,), 0, share_rows).astype(jnp.int32)
    dropped = jax.random.randint(jax.random.fold_in(key, 7), (NBLK,), 0, 10) < 2
    old_row = jnp.where(dropped, drop_row, new_row)
    old_col = jnp.where(dropped, drop_col, new_col)
    return (old_row, old_col, new_row, new_col)


def draw_old_blocks(key, part):
    old_row, old_col, new_row, new_col = block_lists(key)
    return jnp.stack([old_row, old_col], 1).astype(jnp.int32)


def draw_new_blocks(key, part):
    old_row, old_col, new_row, new_col = block_lists(key)
    return jnp.stack([new_row, new_col], 1).astype(jnp.int32)


def draw_new_owner(key, part):
    return owner_targets(key)


def levels(key, extent, cuts, least, largest):
    loudness, own = 1.0, jax.random.fold_in(key, 6)
    for dim, shards_of in cuts:
        heights = jnp.exp(jax.random.uniform(jax.random.fold_in(own, dim), (shards_of,), jnp.float32, least / len(cuts), largest / len(cuts)))
        loudness = loudness * jnp.repeat(heights, extent[dim] // shards_of).reshape([-1 if axis == dim else 1 for axis in range(len(extent))])
    return loudness


def centred(rng, extent, width, limit, shards=(), held_as=jnp.bfloat16):
    values = width * jax.random.normal(rng, extent, jnp.float32)
    if shards:
        values = values * levels(rng, extent, shards, -0.22, 0.18)
    return jnp.clip(values, -limit, limit).astype(held_as)


def setup_inputs(seed: int = 0) -> dict:
    keys = jax.random.split(jax.random.key(seed), 9)
    return {
        "hidden": centred(keys[0], (TOKENS, FF), 1.0, 6.0, ((0, 16), (1, 32))),
        "grad_out": centred(keys[1], (TOKENS, D), 1.0, 6.0, ((0, 16), (1, 32))),
        "old_weight": centred(keys[2], (NBLK, BLOCK, BLOCK), 1.0, 6.0, ((0, 32),)),
        "old_first": centred(keys[3], (NBLK, BLOCK, BLOCK), 0.1, 1.5, ((0, 32),)),
        "old_second": jnp.clip(jnp.exp(math.log(0.19921875) - 3.6901057 * jax.random.uniform(keys[4], (NBLK, BLOCK, BLOCK), jnp.float32) ** levels(keys[4], (NBLK, BLOCK, BLOCK), ((0, 32),), -0.2, 0.2)), 0.0049743652, 0.19921875).astype(jnp.bfloat16),
        "old_blocks": draw_old_blocks(jax.random.fold_in(keys[8], 71), 0),
        "new_blocks": draw_new_blocks(jax.random.fold_in(keys[8], 71), 0),
        "new_owner": draw_new_owner(jax.random.fold_in(keys[8], 71), 0),
    }


beta_one = 0.9
beta_two = 0.95
rate = 0.1
epsilon = 0.1
fix_one = 1.0 - 0.9 ** 10
fix_two = 1.0 - 0.95 ** 10

def adam_update(weight, first, second, grad):
    moment = beta_one * first.astype(jnp.float32) + (1.0 - beta_one) * grad
    square = beta_two * second.astype(jnp.float32) + (1.0 - beta_two) * grad * grad
    change = rate * (moment / fix_one) / (jnp.sqrt(square / fix_two) + epsilon)
    updated = weight.astype(jnp.float32) - change
    return (updated.astype(jnp.bfloat16), moment.astype(jnp.bfloat16), square.astype(jnp.bfloat16))

def reference(hidden, grad_out, old_weight, old_first, old_second, old_blocks, new_blocks, new_owner):
    kept = (old_blocks[:, 0] == new_blocks[:, 0]) & (old_blocks[:, 1] == new_blocks[:, 1])
    onehot = (new_owner[:, None] == jnp.arange(N_OWN, dtype=jnp.int32)[None, :]).astype(jnp.int32)
    before = jnp.cumsum(onehot, 0) - onehot
    rank = lax.optimization_barrier(jnp.sum(before * onehot, 1)).astype(jnp.int32)
    slot = (new_owner * BLK_DEV + rank).astype(jnp.int32)
    keep = kept[:, None, None]
    blank = jnp.zeros_like(old_weight)
    weight = blank.at[slot].set(jnp.where(keep, old_weight, blank))
    first = blank.at[slot].set(jnp.where(keep, old_first, blank))
    second = blank.at[slot].set(jnp.where(keep, old_second, blank))
    rows = jnp.zeros((NBLK,), jnp.int32).at[slot].set(new_blocks[:, 0].astype(jnp.int32))
    cols = jnp.zeros((NBLK,), jnp.int32).at[slot].set(new_blocks[:, 1].astype(jnp.int32))
    scale = (NBLK * BLOCK * BLOCK / D) ** (-0.5)
    placed = (cols[:, None] == jnp.arange(D // BLOCK, dtype=jnp.int32)[None, :]).astype(jnp.float32)
    placed = placed.reshape(N_OWN, BLK_DEV, D // BLOCK)
    weight_wide = weight.astype(jnp.float32)
    hid = hidden.reshape(N_TOK, TOK_GRP, FF)
    cot = grad_out.reshape(N_TOK, TOK_GRP, D)

    def group(total, pair):
        rows_in, cot_in = pair
        picked = jnp.take(rows_in.astype(jnp.float32).reshape(TOK_GRP, FF // BLOCK, BLOCK), rows, axis=1)
        cot_picked = jnp.take(cot_in.astype(jnp.float32).reshape(TOK_GRP, D // BLOCK, BLOCK), cols, axis=1)
        product = jnp.einsum('tjk,jkl->tjl', picked, weight_wide) * scale
        product = product.reshape(TOK_GRP, N_OWN, BLK_DEV, BLOCK)
        partial_value = jnp.einsum('tojl,ojc->otcl', product, placed)
        partial_value = lax.optimization_barrier(partial_value.astype(jnp.bfloat16)).astype(jnp.float32)
        result = lax.optimization_barrier(jnp.sum(partial_value, 0)).reshape(TOK_GRP, D).astype(jnp.bfloat16)
        grad_part = jnp.einsum('tjk,tjl->jkl', picked, cot_picked) * scale
        grad_part = lax.optimization_barrier(grad_part.astype(jnp.bfloat16)).astype(jnp.float32)
        return (total + grad_part, result)
    grad, outs = lax.scan(group, jnp.zeros((NBLK, BLOCK, BLOCK), jnp.float32), (hid, cot))
    output = outs.reshape(TOKENS, D)
    new_weight, new_first, new_second = adam_update(weight, first, second, grad)
    return (output, new_weight, new_first, new_second)
```

```python
import functools

import jax
import jax.numpy as jnp
from jax import lax
from jax.experimental import pallas as pl
from jax.experimental.pallas import tpu as pltpu
from jax.sharding import PartitionSpec as P

MESH = pl.DeviceIdType.MESH

beta_one = 0.9
beta_two = 0.95
rate = 0.1
epsilon = 0.1
fix_one = 1.0 - 0.9**10
fix_two = 1.0 - 0.95**10

BLOCK = 128
ROWS = 8
F32 = jnp.float32
BF16 = jnp.bfloat16


SEND_SLOT = 0
ROW_TILE, ROW_ODD, ROW_KEPT, ROW_ROW, ROW_COL = 1, 2, 3, 4, 5
NEW_TILE, NEW_ODD, NEW_OLD, NEW_ROW, NEW_KEPT = 6, 7, 8, 9, 10
CELL = 11
TABLE_ROWS = 24


def table_kernel(owners, per_dev, row_share, lists_ref, table_ref):
    me = lax.axis_index("own")
    total = lists_ref.shape[0]
    shape = (total, 128)

    def column(i):
        return jnp.broadcast_to(lists_ref[:, i : i + 1], shape)

    owner, old_row, old_col, new_row, new_col = [column(i) for i in range(5)]
    kept = ((old_row == new_row) & (old_col == new_col)).astype(jnp.int32)
    index = lax.broadcasted_iota(jnp.int32, shape, 0)
    lane = lax.broadcasted_iota(jnp.int32, shape, 1)
    row_in = new_row - me * row_share
    row_mine = (row_in >= 0) & (row_in < row_share)
    zero = jnp.zeros(shape, jnp.int32)

    def pick(where, value):
        return jnp.sum(jnp.where(where, value, zero), axis=0, keepdims=True)

    def put(row, value):
        table_ref[row : row + 1, :] = value

    table_ref[...] = jnp.zeros_like(table_ref)
    local = index - me * per_dev
    put(SEND_SLOT, pick((owner == lane) & (local >= 0) & (local < per_dev), local))

    code = ((index * 2 + kept) * 64 + new_col) * 256
    at_row = pick((owner == lane) & row_mine, code + row_in)
    put(ROW_TILE, at_row >> 16)
    put(ROW_ODD, (at_row >> 15) & 1)
    put(ROW_KEPT, (at_row >> 14) & 1)
    put(ROW_COL, (at_row >> 8) & 63)
    put(ROW_ROW, at_row & 255)

    down = lax.broadcasted_iota(jnp.int32, (total, total), 0)
    across = lax.broadcasted_iota(jnp.int32, (total, total), 1)
    earlier = jnp.where(across < down, 1.0, 0.0).astype(BF16)
    mine = owner == me
    rank = jnp.dot(earlier, jnp.where(mine, 1.0, 0.0).astype(BF16), preferred_element_type=F32)
    at_new = pick(mine & (rank.astype(jnp.int32) == lane), (index * 2 + kept) * 256 + new_row)
    new_index = at_new >> 9
    put(NEW_TILE, at_new >> 10)
    put(NEW_ODD, (at_new >> 9) & 1)
    put(NEW_KEPT, (at_new >> 8) & 1)
    old_owner = jnp.zeros_like(at_new)
    row_owner = jnp.zeros_like(at_new)
    for i in range(1, owners):
        old_owner += (new_index >= i * per_dev).astype(jnp.int32)
        row_owner += ((at_new & 255) >= i * row_share).astype(jnp.int32)
    put(NEW_OLD, old_owner)
    put(NEW_ROW, row_owner)

    for r in range(row_share):
        put(CELL + r, owners + pick((row_in == r) & (new_col == lane), owner - owners))


def adam_update(weight, first, second, grad):
    moment = beta_one * first + (1.0 - beta_one) * grad
    square = beta_two * second + (1.0 - beta_two) * grad * grad
    change = rate * (moment / fix_one) / (jnp.sqrt(square / fix_two) + epsilon)
    return weight - change, moment, square


def step_kernel(
    scale,
    table,
    cot,
    hid,
    old_w,
    old_m,
    old_v,
    out_y,
    out_w,
    out_m,
    out_v,
    loc,
    pairs,
    mv_out,
    mv_in,
    cot_all,
    w_all,
    cot_blk,
    hid_t,
    g_out,
    g_in,
    g_sum,
    g_new,
    w_xy,
    w_blk,
    part,
    part_sib,
    right_out,
    right_in,
    left_out,
    left_in,
    fin,
    state,
    loc_sem,
    ring_send,
    ring_recv,
    sib_send,
    sib_recv,
    z_send,
    z_recv,
    xy_send,
    xy_recv,
    rs_send,
    rs_recv,
    pair_send,
    pair_recv,
):
    toks, owners = lax.axis_size("tok"), lax.axis_size("own")
    chips = owners // 2
    t, o = lax.axis_index("tok"), lax.axis_index("own")
    z, core = o // 2, o % 2
    right = {"tok": t, "own": ((z + 1) % chips) * 2 + core}
    left = {"tok": t, "own": ((z + chips - 1) % chips) * 2 + core}
    sibling = {"tok": t, "own": z * 2 + 1 - core}
    per_dev = old_w.shape[0]
    half_dev = per_dev // 2
    row_share = hid_t.shape[0]
    cols = cot_blk.shape[0]
    chunk = cols // chips
    half = BLOCK // 2

    def remote(src, dst, send, recv, device):
        return pltpu.make_async_remote_copy(
            src_ref=src, dst_ref=dst, send_sem=send, recv_sem=recv, device_id=device, device_id_type=MESH
        )

    rows = pl.ds((t // 2) * 16, 16)
    local = [
        pltpu.make_async_copy(old.at[:, rows, :], loc.at[i], loc_sem.at[i])
        for i, old in enumerate((old_w, old_m, old_v))
    ]
    for copy in local:
        copy.start()
    barrier = pltpu.get_barrier_semaphore()

    def greet_z(d, carry):
        pl.semaphore_signal(barrier, inc=1, device_id={"tok": t, "own": (o + d) % owners}, device_id_type=MESH)
        return carry

    def greet_xy(d, carry):
        pl.semaphore_signal(barrier, inc=1, device_id={"tok": (t + d) % toks, "own": o}, device_id_type=MESH)
        return carry

    lax.fori_loop(1, owners, greet_z, 0)
    lax.fori_loop(1, toks, greet_xy, 0)

    cot_all[o] = cot[...]
    for copy in local:
        copy.wait()
    odd_rows = (jnp.zeros((ROWS, BLOCK), jnp.int32) + t % 2) == 1

    def own_rows(i, k):
        both = loc[i, k].astype(F32)
        return jnp.where(odd_rows, both[ROWS:], both[:ROWS])

    def pack_w(p, carry):
        w_all[o * half_dev + p] = jnp.concatenate([own_rows(0, 2 * p), own_rows(0, 2 * p + 1)], 0).astype(BF16)
        return carry

    lax.fori_loop(0, half_dev, pack_w, 0)
    pl.semaphore_wait(barrier, owners - 1 + toks - 1)

    steps = ((chips // 2, chips - 1 - chips // 2), (chips - 1 - chips // 2, chips // 2))

    def shard(b, zz, cc):
        own = (zz % chips) * 2 + cc
        return cot_all.at[own] if b == 0 else w_all.at[pl.ds(own * half_dev, half_dev)]

    def hop(b, way, k):
        zz = z + chips - k if way == 0 else z + k
        ref = shard(b, zz, core)
        return remote(
            ref, ref, ring_send.at[b, way, k], ring_recv.at[b, way, k], right if way == 0 else left
        )

    def aside(b, way, k):
        zz = z + chips - k if way == 0 else z + k
        ref = shard(b, zz, core)
        return remote(ref, ref, sib_send.at[b, way, k], sib_recv.at[b, way, k], sibling)

    for b in range(2):
        for way in range(2):
            if steps[b][way] > 0:
                hop(b, way, 0).start()
    for b in range(2):
        aside(b, 0, 0).start()

    def pack_mv(k, carry):
        pairs[k] = jnp.concatenate([own_rows(1, k), own_rows(2, k)], 0).astype(BF16)
        return carry

    lax.fori_loop(0, per_dev, pack_mv, 0)

    def pick_mv(n, carry):
        mv_out[n] = pairs[table[SEND_SLOT, n]]
        return carry

    lax.fori_loop(0, owners, pick_mv, 0)
    mv_in[o] = mv_out[o]
    for r in range(row_share):
        hid_t[r] = hid[:, r * BLOCK : (r + 1) * BLOCK].astype(F32).T.astype(BF16)
    w_blk[owners] = jnp.zeros((BLOCK, BLOCK), BF16)

    for k in range(chips // 2):
        for b in range(2):
            for way in range(2):
                if k < steps[b][way]:
                    hop(b, way, k).wait_recv()
                    if k + 1 < steps[b][way]:
                        hop(b, way, k + 1).start()
                    aside(b, way, k + 1).start()

    def mv_copy(d):
        to = (o + d) % owners
        return remote(
            mv_out.at[to], mv_in.at[o], z_send.at[0, d], z_recv.at[0, d], {"tok": t, "own": to}
        )

    def start_mv(d, carry):
        mv_copy(d).start()
        return carry

    lax.fori_loop(1, owners, start_mv, 0)

    def wait_aside(b):
        aside(b, 0, 0).wait_recv()
        for way in range(2):
            for k in range(steps[b][way]):
                aside(b, way, k + 1).wait_recv()

    wait_aside(0)
    low = lax.broadcasted_iota(jnp.int32, (half, BLOCK), 1) < half

    def lay_cot(zz, carry):
        first, last = cot_all[2 * zz], cot_all[2 * zz + 1]
        cot_blk[3 * zz] = first[:BLOCK]
        cot_blk[3 * zz + 2] = last[:BLOCK]
        a, b = first[BLOCK:].astype(F32), last[BLOCK:].astype(F32)
        top = jnp.where(low, a, pltpu.roll(b, half, 1))
        bottom = jnp.where(low, pltpu.roll(a, half, 1), b)
        cot_blk[3 * zz + 1] = jnp.concatenate([top, bottom], 0).astype(BF16)
        return carry

    lax.fori_loop(0, chips, lay_cot, 0)

    def grad_pair(k, carry):
        slices = []
        for n in (2 * k, 2 * k + 1):
            g = jnp.dot(hid_t[table[ROW_ROW, n]], cot_blk[table[ROW_COL, n]], preferred_element_type=F32)
            slices.append((g * scale).reshape(toks, ROWS, BLOCK))
        g_out[:, k] = jnp.concatenate(slices, 1).astype(BF16)
        return carry

    lax.fori_loop(0, owners // 2, grad_pair, 0)

    def g_copy(d):
        to = (t + d) % toks
        return remote(g_out.at[to], g_in.at[t], xy_send.at[0, d], xy_recv.at[0, d], {"tok": to, "own": o})

    def start_g(d, carry):
        g_copy(d).start()
        return carry

    lax.fori_loop(1, toks, start_g, 0)
    g_in[t] = g_out[t]

    wait_aside(1)

    def rows_of(tile, odd):
        both = w_all[tile].astype(F32)
        return jnp.where((jnp.zeros((ROWS, BLOCK), jnp.int32) + odd) == 1, both[ROWS:], both[:ROWS])

    def pick_w(k, carry):
        parts = []
        for n in (2 * k, 2 * k + 1):
            parts.append(rows_of(table[ROW_TILE, n], table[ROW_ODD, n]) * table[ROW_KEPT, n].astype(F32))
        w_xy[t, k] = jnp.concatenate(parts, 0).astype(BF16)
        return carry

    lax.fori_loop(0, owners // 2, pick_w, 0)

    def w_copy(d):
        to = (t + d) % toks
        return remote(w_xy.at[t], w_xy.at[t], xy_send.at[1, d], xy_recv.at[1, d], {"tok": to, "own": o})

    def start_w(d, carry):
        w_copy(d).start()
        return carry

    lax.fori_loop(1, toks, start_w, 0)

    def wait_g(d, carry):
        g_copy(d).wait_recv()
        return carry

    lax.fori_loop(1, toks, wait_g, 0)

    def sum_g(k, carry):
        total = jnp.sum(g_in[:, k].astype(F32), axis=0)
        g_sum[2 * k] = total[:ROWS]
        g_sum[2 * k + 1] = total[ROWS:]
        return carry

    lax.fori_loop(0, owners // 2, sum_g, 0)

    def gz_copy(d):
        to = (o + d) % owners
        return remote(
            g_sum.at[to], g_new.at[o], z_send.at[1, d], z_recv.at[1, d], {"tok": t, "own": to}
        )

    def start_gz(d, carry):
        gz_copy(d).start()
        return carry

    lax.fori_loop(1, owners, start_gz, 0)
    g_new[o] = g_sum[o]

    def wait_w(d, carry):
        w_copy(d).wait_recv()
        return carry

    lax.fori_loop(1, toks, wait_w, 0)

    def lay_w(k, carry):
        both = w_xy[:, k].astype(F32)
        w_blk[2 * k] = both[:, :ROWS].reshape(BLOCK, BLOCK).astype(BF16)
        w_blk[2 * k + 1] = both[:, ROWS:].reshape(BLOCK, BLOCK).astype(BF16)
        return carry

    lax.fori_loop(0, owners // 2, lay_w, 0)

    def product(q, carry):
        total = jnp.zeros((BLOCK, 2 * BLOCK), F32)
        for r in range(0, row_share, 2):
            wide = jnp.concatenate(
                [
                    jnp.concatenate([w_blk[table[CELL + r + i, 2 * q + j]] for j in range(2)], 1)
                    for i in range(2)
                ],
                0,
            )
            total += jnp.dot(hid[:, r * BLOCK : (r + 2) * BLOCK], wide, preferred_element_type=F32)
        total = (total * scale).astype(BF16)
        for i in range(2):
            for j in range(2):
                part[i, 2 * q + j] = total[i * half : (i + 1) * half, j * BLOCK : (j + 1) * BLOCK]
        return carry

    lax.fori_loop(0, cols // 2, product, 0)
    swap = remote(part.at[1 - core], part_sib, pair_send.at[0], pair_recv.at[0], sibling)
    swap.start()

    def wait_z(d, carry):
        mv_copy(d).wait_recv()
        gz_copy(d).wait_recv()
        return carry

    lax.fori_loop(1, owners, wait_z, 0)

    def adam_pair(p, carry):
        results = []
        for s in (2 * p, 2 * p + 1):
            kept = table[NEW_KEPT, s].astype(F32)
            w = rows_of(table[NEW_TILE, s], table[NEW_ODD, s]) * kept
            both = mv_in[table[NEW_OLD, s]].astype(F32) * kept
            results.append(adam_update(w, both[:ROWS], both[ROWS:], g_new[table[NEW_ROW, s]]))
        for i in range(3):
            state[t, i, p] = jnp.concatenate([r[i] for r in results], 0).astype(BF16)
        return carry

    lax.fori_loop(0, half_dev, adam_pair, 0)

    def state_copy(i, d):
        to = (t + d) % toks
        return remote(
            state.at[t, i], state.at[t, i], xy_send.at[2 + i, d], xy_recv.at[2 + i, d], {"tok": to, "own": o}
        )

    for i in range(3):

        def start_state(d, carry, i=i):
            state_copy(i, d).start()
            return carry

        lax.fori_loop(1, toks, start_state, 0)

    swap.wait_recv()

    def term(zz):
        at = pl.ds((zz % chips) * chunk, chunk)
        return part[core, at].astype(F32) + part_sib[at].astype(F32)

    to_right, to_left = steps[0]

    def rs_copy(way, k):
        if way == 0:
            return remote(right_out.at[k], right_in.at[k], rs_send.at[0, k], rs_recv.at[0, k], right)
        return remote(left_out.at[k], left_in.at[k], rs_send.at[1, k], rs_recv.at[1, k], left)

    for k in range(to_right):
        value = term(z + to_right - k)
        if k > 0:
            rs_copy(0, k - 1).wait_recv()
            value += right_in[k - 1].astype(F32)
        right_out[k] = value.astype(BF16)
        rs_copy(0, k).start()
        if k < to_left:
            value = term(z + chips - to_left + k)
            if k > 0:
                rs_copy(1, k - 1).wait_recv()
                value += left_in[k - 1].astype(F32)
            left_out[k] = value.astype(BF16)
            rs_copy(1, k).start()
    value = term(z)
    rs_copy(0, to_right - 1).wait_recv()
    value += right_in[to_right - 1].astype(F32)
    if to_left > 0:
        rs_copy(1, to_left - 1).wait_recv()
        value += left_in[to_left - 1].astype(F32)
    fin[core] = value.astype(BF16)
    finish = remote(fin.at[core], fin.at[core], pair_send.at[1], pair_recv.at[1], sibling)
    finish.start()

    for i, result in enumerate((out_w, out_m, out_v)):

        def wait_state(d, carry, i=i):
            state_copy(i, d).wait_recv()
            return carry

        lax.fori_loop(1, toks, wait_state, 0)

        def lay_state(p, carry, i=i, result=result):
            both = state[:, i, p].astype(F32)
            result[2 * p] = both[:, :ROWS].reshape(BLOCK, BLOCK).astype(BF16)
            result[2 * p + 1] = both[:, ROWS:].reshape(BLOCK, BLOCK).astype(BF16)
            return carry

        lax.fori_loop(0, half_dev, lay_state, 0)
    finish.wait_recv()
    out_y[...] = fin[...]

    for b in range(2):
        aside(b, 0, 0).wait_send()
        for way in range(2):
            for k in range(steps[b][way]):
                hop(b, way, k).wait_send()
                aside(b, way, k + 1).wait_send()

    def sent_z(d, carry):
        mv_copy(d).wait_send()
        gz_copy(d).wait_send()
        return carry

    def sent_xy(d, carry):
        g_copy(d).wait_send()
        w_copy(d).wait_send()
        for i in range(3):
            state_copy(i, d).wait_send()
        return carry

    lax.fori_loop(1, owners, sent_z, 0)
    lax.fori_loop(1, toks, sent_xy, 0)
    for k in range(to_right):
        rs_copy(0, k).wait_send()
    for k in range(to_left):
        rs_copy(1, k).wait_send()
    swap.wait_send()
    finish.wait_send()


def local(hidden, grad_out, old_weight, old_first, old_second, old_blocks, new_blocks, new_owner):
    owners, toks = lax.axis_size("own"), lax.axis_size("tok")
    chips = owners // 2
    core = lax.axis_index("own") % 2
    per_dev, block = old_weight.shape[0], old_weight.shape[1]
    total = new_owner.shape[0]
    tokens = hidden.shape[0]
    row_share = hidden.shape[1] // block
    width = grad_out.shape[1] * owners
    cols = width // block
    chunk = cols // chips
    half = block // 2
    scale = (total * block * block / width) ** (-0.5)

    lists = jnp.concatenate([new_owner[:, None], old_blocks, new_blocks], axis=1)
    table = pl.pallas_call(
        functools.partial(table_kernel, owners, per_dev, row_share),
        out_shape=jax.ShapeDtypeStruct((TABLE_ROWS, 128), jnp.int32),
        in_specs=[pl.BlockSpec(memory_space=pltpu.VMEM)],
        out_specs=pl.BlockSpec(memory_space=pltpu.VMEM),
        compiler_params=pltpu.CompilerParams(vmem_limit_bytes=32 * 2**20),
        name="block_table",
    )(lists)

    whole = jnp.where(core == 0, grad_out[:, :block], grad_out[:, half:])
    part = jnp.where(core == 0, grad_out[:, block:], grad_out[:, :half])
    cot = jnp.concatenate([whole, jnp.concatenate([part[:half], part[half:]], 1)], 0)

    vmem = pl.BlockSpec(memory_space=pltpu.VMEM)
    hbm = pl.BlockSpec(memory_space=pl.ANY)
    dma = pltpu.SemaphoreType.DMA
    ring = chips // 2
    piece = (chunk, half, block)
    state_shape = jax.ShapeDtypeStruct(old_weight.shape, BF16)
    y, new_weight, new_first, new_second = pl.pallas_call(
        functools.partial(step_kernel, scale),
        out_shape=(jax.ShapeDtypeStruct((2,) + piece, BF16), state_shape, state_shape, state_shape),
        in_specs=[pl.BlockSpec(memory_space=pltpu.SMEM), vmem, vmem, hbm, hbm, hbm],
        out_specs=(vmem, vmem, vmem, vmem),
        scratch_shapes=[
            pltpu.VMEM((3, per_dev, 16, block), BF16),
            pltpu.VMEM((per_dev, 16, block), BF16),
            pltpu.VMEM((owners, 16, block), BF16),
            pltpu.VMEM((owners, 16, block), BF16),
            pltpu.VMEM((owners, block + half, block), BF16),
            pltpu.VMEM((total // 2, 16, block), BF16),
            pltpu.VMEM((cols, tokens, block), BF16),
            pltpu.VMEM((row_share, block, tokens), BF16),
            pltpu.VMEM((toks, owners // 2, 16, block), BF16),
            pltpu.VMEM((toks, owners // 2, 16, block), BF16),
            pltpu.VMEM((owners, ROWS, block), F32),
            pltpu.VMEM((owners, ROWS, block), F32),
            pltpu.VMEM((toks, owners // 2, 16, block), BF16),
            pltpu.VMEM((owners + 1, block, block), BF16),
            pltpu.VMEM((2, cols, half, block), BF16),
            pltpu.VMEM((cols, half, block), BF16),
            pltpu.VMEM((ring,) + piece, BF16),
            pltpu.VMEM((ring,) + piece, BF16),
            pltpu.VMEM((ring,) + piece, BF16),
            pltpu.VMEM((ring,) + piece, BF16),
            pltpu.VMEM((2,) + piece, BF16),
            pltpu.VMEM((toks, 3, per_dev // 2, 16, block), BF16),
            dma((3,)),
            dma((2, 2, ring)),
            dma((2, 2, ring)),
            dma((2, 2, ring + 1)),
            dma((2, 2, ring + 1)),
            dma((2, owners)),
            dma((2, owners)),
            dma((5, toks)),
            dma((5, toks)),
            dma((2, ring)),
            dma((2, ring)),
            dma((2,)),
            dma((2,)),
        ],
        compiler_params=pltpu.CompilerParams(
            collective_id=0, has_side_effects=True, vmem_limit_bytes=48 * 2**20
        ),
        name="projection_step",
    )(table, cot, hidden, old_weight, old_first, old_second)

    y = y.transpose(0, 2, 1, 3).reshape(tokens, chunk * block)
    output = lax.dynamic_slice_in_dim(y, core * grad_out.shape[1], grad_out.shape[1], 1)
    return (output, new_weight, new_first, new_second)


def solution(mesh):
    state = P("own", None, None)
    in_specs = (P("tok", "own"), P("tok", "own"), state, state, state, P(), P(), P())
    out_specs = (P("tok", "own"), state, state, state)
    return jax.shard_map(local, mesh=mesh, in_specs=in_specs, out_specs=out_specs, check_vma=False)
```

```python
import functools

import jax
import jax.numpy as jnp
from jax import lax
from jax.experimental import pallas as pl
from jax.experimental.pallas import tpu as pltpu
from jax.sharding import PartitionSpec as P

MESH = pl.DeviceIdType.MESH

beta_one = 0.9
beta_two = 0.95
rate = 0.1
epsilon = 0.1
fix_one = 1.0 - 0.9**10
fix_two = 1.0 - 0.95**10

BLOCK = 128
ROWS = 8
F32 = jnp.float32
BF16 = jnp.bfloat16


SEND_SLOT = 0
HOP_OLD, HOP_KEPT = 1, 2
ROW_ROW, ROW_COL = 3, 4
NEW_OLD, NEW_ROW, NEW_KEPT = 5, 6, 7
CELL = 8
TABLE_ROWS = 16


def table_kernel(owners, per_dev, row_share, lists_ref, table_ref):
    me = lax.axis_index("own")
    total = lists_ref.shape[0]
    shape = (total, 128)

    def column(i):
        return jnp.broadcast_to(lists_ref[:, i : i + 1], shape)

    owner, old_row, old_col, new_row, new_col = [column(i) for i in range(5)]
    kept = ((old_row == new_row) & (old_col == new_col)).astype(jnp.int32)
    index = lax.broadcasted_iota(jnp.int32, shape, 0)
    lane = lax.broadcasted_iota(jnp.int32, shape, 1)
    row_in = new_row - me * row_share
    row_mine = (row_in >= 0) & (row_in < row_share)
    zero = jnp.zeros(shape, jnp.int32)

    def pick(where, value):
        return jnp.sum(jnp.where(where, value, zero), axis=0, keepdims=True)

    def put(row, value):
        table_ref[row : row + 1, :] = value

    def place(value, share):
        own = jnp.zeros_like(value)
        for i in range(1, owners):
            own += (value >= i * share).astype(jnp.int32)
        return (own & 1) * (owners // 2) + (own >> 1)

    table_ref[...] = jnp.zeros_like(table_ref)
    local = index - me * per_dev
    put(SEND_SLOT, pick((owner == lane) & (local >= 0) & (local < per_dev), local))

    mine = owner == me
    row_at = new_row - lane * row_share
    hop = pick(mine & (row_at >= 0) & (row_at < row_share), index * 2 + kept)
    put(HOP_OLD, place(hop >> 1, per_dev))
    put(HOP_KEPT, hop & 1)

    at_row = pick((owner == lane) & row_mine, new_col * 256 + row_in)
    put(ROW_COL, at_row >> 8)
    put(ROW_ROW, at_row & 255)

    down = lax.broadcasted_iota(jnp.int32, (total, total), 0)
    across = lax.broadcasted_iota(jnp.int32, (total, total), 1)
    earlier = jnp.where(across < down, 1.0, 0.0).astype(BF16)
    rank = jnp.dot(earlier, jnp.where(mine, 1.0, 0.0).astype(BF16), preferred_element_type=F32)
    at_new = pick(mine & (rank.astype(jnp.int32) == lane), (index * 2 + kept) * 256 + new_row)
    put(NEW_OLD, place(at_new >> 9, per_dev))
    put(NEW_ROW, place(at_new & 255, row_share))
    put(NEW_KEPT, (at_new >> 8) & 1)

    for r in range(row_share):
        put(CELL + r, owners + pick((row_in == r) & (new_col == lane), owner - owners))


def adam_update(weight, first, second, grad):
    moment = beta_one * first + (1.0 - beta_one) * grad
    square = beta_two * second + (1.0 - beta_two) * grad * grad
    change = rate * (moment / fix_one) / (jnp.sqrt(square / fix_two) + epsilon)
    return weight - change, moment, square


JUMP = 5


def step_kernel(
    scale,
    table,
    cot,
    hid,
    old_w,
    old_m,
    old_v,
    out_y,
    out_w,
    out_m,
    out_v,
    loc_w,
    loc_m,
    loc_v,
    w1_out,
    w1_in,
    w2_out,
    w2_in,
    mv_out,
    mv_in,
    cot_all,
    cot_blk,
    hid_b,
    hid_t,
    g_out,
    g_one,
    g_mid,
    g_two,
    g_sum,
    g_new,
    g_all,
    w_all,
    state,
    prod,
    part,
    part_sib,
    rs_out,
    rs_in,
    fin,
    loc_sem,
    cot_send,
    cot_recv,
    sib_send,
    sib_recv,
    z_send,
    z_recv,
    fwd_send,
    fwd_recv,
    xy_send,
    xy_recv,
    rs_send,
    rs_recv,
):
    toks, owners = lax.axis_size("tok"), lax.axis_size("own")
    side = 4
    chips = owners // 2
    t, o = lax.axis_index("tok"), lax.axis_index("own")
    z, core = o // 2, o % 2
    y, x = t // side, t % side
    sibling = {"tok": t, "own": z * 2 + 1 - core}
    per_dev = old_w.shape[0]
    half_dev = per_dev // 2
    row_share = hid_t.shape[0]
    cols = cot_blk.shape[0]
    chunk = cols // chips
    half = BLOCK // 2
    pairs = owners // 2
    reach = (chips // 2, chips - 1 - chips // 2)

    def remote(src, dst, send, recv, device):
        return pltpu.make_async_remote_copy(
            src_ref=src, dst_ref=dst, send_sem=send, recv_sem=recv, device_id=device, device_id_type=MESH
        )

    def along_z(d):
        return {"tok": t, "own": ((z + d) % chips) * 2 + core}

    def tok_at(dy, dx):
        return ((y + dy) % side) * side + (x + dx) % side

    def across(dy, dx):
        return {"tok": tok_at(dy, dx), "own": o}

    def loop(first, last, body):
        def step(i, carry):
            body(i)
            return carry

        lax.fori_loop(first, last, step, 0)

    loc = (loc_w, loc_m, loc_v)

    rows = pl.ds((t // 2) * 16, 16)
    local = [
        pltpu.make_async_copy(old.at[:, rows, :], loc[i], loc_sem.at[i])
        for i, old in enumerate((old_w, old_m, old_v))
    ]
    for copy in local:
        copy.start()
    barrier = pltpu.get_barrier_semaphore()

    def greet(device):
        pl.semaphore_signal(barrier, inc=1, device_id=device, device_id_type=MESH)

    greet(sibling)
    loop(1, chips, lambda d: greet(along_z(d)))
    loop(1, side, lambda d: greet(across(0, d)))
    loop(1, side, lambda d: greet(across(d, 0)))

    def is_one(bit):
        return (jnp.zeros((ROWS, BLOCK), jnp.int32) + bit) == 1

    odd_rows, second_core = is_one(t % 2), is_one(core)

    def own_rows(i, k):
        both = loc[i][k].astype(F32)
        return jnp.where(odd_rows, both[ROWS:], both[:ROWS])

    def core_rows(tile):
        both = tile.astype(F32)
        return jnp.where(second_core, both[ROWS:], both[:ROWS])

    def stack(a, b):
        return jnp.concatenate([a, b], 0).astype(BF16)

    cot_all[o] = cot[...]
    local[0].wait()

    def pack_w1(k):
        w1_out[k] = stack(own_rows(0, table[SEND_SLOT, 2 * k]), own_rows(0, table[SEND_SLOT, 2 * k + 1]))

    loop(0, chips, pack_w1)
    pl.semaphore_wait(barrier, chips - 1 + 1 + 2 * (side - 1))

    def cot_at(way, distance):
        zz = z + chips - distance if way == 0 else z + distance
        return cot_all.at[(zz % chips) * 2 + core]

    def cot_hop(way, distance):
        step = distance if distance in (1, JUMP) else 1
        ref = cot_at(way, distance - step)
        return remote(
            ref,
            ref,
            cot_send.at[way, distance],
            cot_recv.at[way, distance],
            along_z(step if way == 0 else chips - step),
        )

    def cot_aside(way, distance):
        ref = cot_at(way, distance)
        return remote(ref, ref, sib_send.at[way, distance], sib_recv.at[way, distance], sibling)

    def cot_step(distance):
        for way in range(2):
            if distance <= reach[way]:
                cot_hop(way, distance).wait_recv()
                if distance + 1 <= reach[way] and distance + 1 != JUMP:
                    cot_hop(way, distance + 1).start()
                cot_aside(way, distance).start()

    def far_first(i):
        return chips // 2 + ((i + 1) // 2) * (1 - 2 * (i % 2))

    def z_copy(plane, src, dst, d):
        zz = (z + d) % chips
        return remote(
            src(zz),
            dst.at[core * chips + z],
            z_send.at[plane, d],
            z_recv.at[plane, d],
            {"tok": t, "own": zz * 2 + core},
        )

    def forward(plane, ref):
        return remote(ref, ref, fwd_send.at[plane], fwd_recv.at[plane], sibling)

    my_chips = pl.ds(core * chips, chips)
    z_all = {
        "w1": (0, lambda zz: w1_out.at[zz], w1_in),
        "mv": (1, lambda zz: mv_out.at[pl.ds(2 * zz, 2)], mv_in),
        "w2": (2, lambda zz: w2_out.at[zz], w2_in),
        "g": (3, lambda zz: g_sum.at[zz], g_new),
    }
    fwd = {
        "w1": forward(0, w1_in.at[my_chips]),
        "mv": forward(1, mv_in.at[my_chips, 1 - core]),
        "w2": forward(2, w2_in.at[my_chips]),
        "g": forward(3, g_new.at[my_chips]),
    }

    def z_start(name):
        loop(0, chips - 1, lambda i: z_copy(*z_all[name], far_first(i)).start())

    def z_wait(name):
        loop(1, chips, lambda d: z_copy(*z_all[name], d).wait_recv())
        fwd[name].start()

    def xy_one(plane, at, h, d):
        ref = at(h, t)
        to = across(0, d) if h == 0 else across(d, 0)
        return remote(ref, ref, xy_send.at[plane, h, 0, d], xy_recv.at[plane, h, 0, d], to)

    def xy_two(plane, at, h, e, d):
        ref = at(h, tok_at(0, e) if h == 0 else tok_at(e, 0))
        to = across(d, 0) if h == 0 else across(0, d)
        return remote(ref, ref, xy_send.at[plane, h, 1 + e, d], xy_recv.at[plane, h, 1 + e, d], to)

    def ag_start(plane, at):
        for h in range(2):
            loop(1, side, lambda d: xy_one(plane, at, h, d).start())
        for h in range(2):
            loop(1, side, lambda d: xy_two(plane, at, h, 0, d).start())

    def ag_pass_on(plane, at):
        def pass_on(d):
            for h in range(2):
                xy_one(plane, at, h, d).wait_recv()
                loop(1, side, lambda dd: xy_two(plane, at, h, side - d, dd).start())

        loop(1, side, pass_on)

    def ag_each(plane, at, do):
        for h in range(2):
            loop(0, side, lambda e: loop(1, side, lambda d: do(xy_two(plane, at, h, e, d))))

    def ag_wait(plane, at):
        ag_each(plane, at, lambda copy: copy.wait_recv())

    def ag_sent(plane, at):
        for h in range(2):
            loop(1, side, lambda d: xy_one(plane, at, h, d).wait_send())
        ag_each(plane, at, lambda copy: copy.wait_send())

    def halves(ref):
        n = ref.shape[1] // 2
        return lambda h, i: ref.at[i, pl.ds(h * n, n)]

    ag_w, ag_state, ag_g = (0, halves(w_all)), (1, halves(state)), (2, halves(g_all))

    for way in range(2):
        cot_hop(way, 1).start()
    for way in range(2):
        if JUMP <= reach[way]:
            cot_hop(way, JUMP).start()
    z_start("w1")
    cot_aside(0, 0).start()
    w1_in[core * chips + z] = w1_out[z]

    for i in (1, 2):
        local[i].wait()

    def pack_mv(n):
        k = table[SEND_SLOT, n]
        mv_out[n] = stack(own_rows(1, k), own_rows(2, k))

    loop(0, owners, pack_mv)
    z_start("mv")
    mv_in[core * chips + z] = mv_out[pl.ds(2 * z, 2)]

    for r in range(row_share):
        block = hid[:, r * BLOCK : (r + 1) * BLOCK]
        hid_b[r] = block
        hid_t[r] = block.astype(F32).T.astype(BF16)
    prod[owners] = jnp.zeros(prod.shape[1:], F32)

    for distance in (1, 5, 2, 6):
        cot_step(distance)
    z_wait("w1")
    cot_step(3)
    fwd["w1"].wait_recv()

    def pack_w2(k):
        parts = []
        for r in (2 * k, 2 * k + 1):
            parts.append(core_rows(w1_in[table[HOP_OLD, r]]) * table[HOP_KEPT, r].astype(F32))
        w2_out[k] = stack(*parts)

    loop(0, chips, pack_w2)
    z_start("w2")
    w2_in[core * chips + z] = w2_out[z]
    for distance in (7, 4, 8):
        cot_step(distance)
    z_wait("mv")

    cot_aside(0, 0).wait_recv()
    for way in range(2):
        for distance in range(1, reach[way] + 1):
            cot_aside(way, distance).wait_recv()

    low = lax.broadcasted_iota(jnp.int32, (half, BLOCK), 1) < half

    def lay_cot(zz):
        first, last = cot_all[2 * zz], cot_all[2 * zz + 1]
        cot_blk[3 * zz] = first[:BLOCK]
        cot_blk[3 * zz + 2] = last[:BLOCK]
        a, b = first[BLOCK:].astype(F32), last[BLOCK:].astype(F32)
        top = jnp.where(low, a, pltpu.roll(b, half, 1))
        bottom = jnp.where(low, pltpu.roll(a, half, 1), b)
        cot_blk[3 * zz + 1] = stack(top, bottom)

    loop(0, chips, lay_cot)

    def grad_pair(k):
        slices = []
        for n in (2 * k, 2 * k + 1):
            g = jnp.dot(hid_t[table[ROW_ROW, n]], cot_blk[table[ROW_COL, n]], preferred_element_type=F32)
            slices.append((g * scale).reshape(toks, ROWS, BLOCK))
        g_out[:, k] = jnp.concatenate(slices, 1).astype(BF16)

    loop(0, pairs, grad_pair)

    def half_pairs(h):
        return pl.ds(h * (pairs // 2), pairs // 2)

    def g_first(h, e, d):
        to = tok_at(e, d) if h == 0 else tok_at(d, e)
        return remote(
            g_out.at[to, half_pairs(h)],
            g_one.at[h, d, e],
            xy_send.at[3, h, 1 + e, d],
            xy_recv.at[3, h, 1 + e, d],
            across(0, d) if h == 0 else across(d, 0),
        )

    def g_second(h, e):
        return remote(
            g_mid.at[h, e],
            g_two.at[h, e],
            xy_send.at[3, h, 0, e],
            xy_recv.at[3, h, 0, e],
            across(e, 0) if h == 0 else across(0, e),
        )

    def g_each(do):
        for h in range(2):
            loop(1, side, lambda e: loop(1, side, lambda d: do(g_first(h, e, d))))
        for h in range(2):
            loop(1, side, lambda d: do(g_first(h, 0, d)))

    g_each(lambda copy: copy.start())

    fwd["mv"].wait_recv()

    def pack_state(p):
        parts = []
        for s in (2 * p, 2 * p + 1):
            kept = table[NEW_KEPT, s].astype(F32)
            place = table[NEW_OLD, s]
            both = mv_in[place, core].astype(F32) * kept
            parts.append((core_rows(w1_in[place]) * kept, both[:ROWS], both[ROWS:]))
        for i in range(3):
            state[t, i * half_dev + p] = stack(parts[0][i], parts[1][i])

    loop(0, half_dev, pack_state)

    z_wait("w2")
    fwd["w2"].wait_recv()

    def pack_w(k):
        w_all[t, k] = stack(core_rows(w2_in[k]), core_rows(w2_in[chips + k]))

    loop(0, pairs, pack_w)
    ag_start(*ag_w)
    ag_pass_on(*ag_w)
    ag_start(*ag_state)

    def g_middle(e):
        for h in range(2):
            loop(1, side, lambda d: g_first(h, e, d).wait_recv())
            own = g_out[tok_at(e, 0) if h == 0 else tok_at(0, e), half_pairs(h)].astype(F32)
            others = [g_one[h, d, e].astype(F32) for d in range(1, side)]
            g_mid[h, e] = (own + others[0] + others[1] + others[2]).astype(BF16)

    def g_on(e):
        g_middle(e)
        for h in range(2):
            g_second(h, e).start()

    loop(1, side, g_on)
    g_middle(0)
    for h in range(2):
        loop(1, side, lambda e: g_second(h, e).wait_recv())
        total = g_mid[h, 0].astype(F32)
        for e in range(1, side):
            total += g_two[h, e].astype(F32)
        g_sum[half_pairs(h)] = total.astype(BF16)
    z_start("g")
    g_new[core * chips + z] = g_sum[z]
    ag_pass_on(*ag_state)

    ag_wait(*ag_w)

    def product(k):
        both = w_all[:, k].astype(F32)
        for i in range(2):
            n = 2 * k + i
            w = both[:, i * ROWS : (i + 1) * ROWS].reshape(BLOCK, BLOCK).astype(BF16)
            p = jnp.dot(hid_b[table[ROW_ROW, n]], w, preferred_element_type=F32) * scale
            prod[n] = p.reshape(2, half, BLOCK)

    loop(0, pairs, product)

    def gather_part(h):
        def column(c):
            total = prod[table[CELL, c], h]
            for r in range(1, row_share):
                total += prod[table[CELL + r, c], h]
            part[h, c] = total.astype(BF16)

        loop(0, cols, column)

    gather_part(1 - core)
    swap = remote(part.at[1 - core], part_sib, fwd_send.at[4], fwd_recv.at[4], sibling)
    swap.start()
    gather_part(core)
    swap.wait_recv()

    def term(zz):
        at = pl.ds((zz % chips) * chunk, chunk)
        return part[core, at].astype(F32) + part_sib[at].astype(F32)

    def rs_hop(way, distance):
        step = JUMP if distance == JUMP else 1
        return remote(
            rs_out.at[way, distance],
            rs_in.at[way, distance],
            rs_send.at[way, distance],
            rs_recv.at[way, distance],
            along_z(step if way == 0 else chips - step),
        )

    def rs_step(way, distance):
        if distance > reach[way]:
            return
        value = term(z + distance if way == 0 else z + chips - distance)
        if distance not in (JUMP - 1, reach[way]):
            rs_hop(way, distance + 1).wait_recv()
            value += rs_in[way, distance + 1].astype(F32)
        rs_out[way, distance] = value.astype(BF16)
        rs_hop(way, distance).start()

    def rs_round(k):
        for way in range(2):
            if reach[way] - k >= JUMP:
                rs_step(way, reach[way] - k)
        for way in range(2):
            if JUMP - 1 - k >= 1:
                rs_step(way, min(JUMP - 1, reach[way]) - k)

    rs_round(0)

    z_wait("g")
    fwd["g"].wait_recv()

    def pack_g(p):
        g_all[t, p] = stack(*[core_rows(g_new[table[NEW_ROW, s]]) for s in (2 * p, 2 * p + 1)])

    loop(0, half_dev, pack_g)
    ag_start(*ag_g)
    rs_round(1)
    ag_pass_on(*ag_g)
    rs_round(2)
    rs_round(3)

    ag_wait(*ag_state)
    ag_wait(*ag_g)

    def adam(p):
        g, w, m, v = [
            ref[:, i].astype(F32)
            for ref, i in ((g_all, p), (state, p), (state, half_dev + p), (state, 2 * half_dev + p))
        ]
        for result, value in zip((out_w, out_m, out_v), adam_update(w, m, v, g)):
            for i in range(2):
                part_rows = value[:, i * ROWS : (i + 1) * ROWS]
                result[2 * p + i] = part_rows.reshape(BLOCK, BLOCK).astype(BF16)

    loop(0, half_dev, adam)

    value = term(z)
    for way in range(2):
        for distance in (1, JUMP):
            if distance <= reach[way]:
                rs_hop(way, distance).wait_recv()
                value += rs_in[way, distance].astype(F32)
    fin[core] = value.astype(BF16)
    finish = remote(fin.at[core], fin.at[core], fwd_send.at[5], fwd_recv.at[5], sibling)
    finish.start()
    finish.wait_recv()
    out_y[...] = fin[...]

    cot_aside(0, 0).wait_send()
    for way in range(2):
        for distance in range(1, reach[way] + 1):
            cot_hop(way, distance).wait_send()
            cot_aside(way, distance).wait_send()
            rs_hop(way, distance).wait_send()
    for name in z_all:
        loop(1, chips, lambda d: z_copy(*z_all[name], d).wait_send())
        fwd[name].wait_send()
    for gather in (ag_w, ag_state, ag_g):
        ag_sent(*gather)
    g_each(lambda copy: copy.wait_send())
    for h in range(2):
        loop(1, side, lambda e: g_second(h, e).wait_send())
    swap.wait_send()
    finish.wait_send()


def local(hidden, grad_out, old_weight, old_first, old_second, old_blocks, new_blocks, new_owner):
    owners, toks = lax.axis_size("own"), lax.axis_size("tok")
    chips = owners // 2
    core = lax.axis_index("own") % 2
    per_dev, block = old_weight.shape[0], old_weight.shape[1]
    total = new_owner.shape[0]
    tokens = hidden.shape[0]
    row_share = hidden.shape[1] // block
    width = grad_out.shape[1] * owners
    cols = width // block
    chunk = cols // chips
    half = block // 2
    scale = (total * block * block / width) ** (-0.5)

    lists = jnp.concatenate([new_owner[:, None], old_blocks, new_blocks], axis=1)
    table = pl.pallas_call(
        functools.partial(table_kernel, owners, per_dev, row_share),
        out_shape=jax.ShapeDtypeStruct((TABLE_ROWS, 128), jnp.int32),
        in_specs=[pl.BlockSpec(memory_space=pltpu.VMEM)],
        out_specs=pl.BlockSpec(memory_space=pltpu.VMEM),
        compiler_params=pltpu.CompilerParams(vmem_limit_bytes=32 * 2**20),
        name="block_table",
    )(lists)

    whole = jnp.where(core == 0, grad_out[:, :block], grad_out[:, half:])
    part = jnp.where(core == 0, grad_out[:, block:], grad_out[:, :half])
    cot = jnp.concatenate([whole, jnp.concatenate([part[:half], part[half:]], 1)], 0)

    vmem = pl.BlockSpec(memory_space=pltpu.VMEM)
    hbm = pl.BlockSpec(memory_space=pl.ANY)
    dma = pltpu.SemaphoreType.DMA
    ring = chips // 2
    piece = (chunk, half, block)
    state_shape = jax.ShapeDtypeStruct(old_weight.shape, BF16)
    y, new_weight, new_first, new_second = pl.pallas_call(
        functools.partial(step_kernel, scale),
        out_shape=(jax.ShapeDtypeStruct((2,) + piece, BF16), state_shape, state_shape, state_shape),
        in_specs=[pl.BlockSpec(memory_space=pltpu.SMEM), vmem, vmem, hbm, hbm, hbm],
        out_specs=(vmem, vmem, vmem, vmem),
        scratch_shapes=[
            pltpu.VMEM((per_dev, 16, block), BF16),
            pltpu.VMEM((per_dev, 16, block), BF16),
            pltpu.VMEM((per_dev, 16, block), BF16),
            pltpu.VMEM((chips, 16, block), BF16),
            pltpu.VMEM((owners, 16, block), BF16),
            pltpu.VMEM((chips, 16, block), BF16),
            pltpu.VMEM((owners, 16, block), BF16),
            pltpu.VMEM((owners, 16, block), BF16),
            pltpu.VMEM((owners, 2, 16, block), BF16),
            pltpu.VMEM((owners, block + half, block), BF16),
            pltpu.VMEM((cols, tokens, block), BF16),
            pltpu.VMEM((row_share, tokens, block), BF16),
            pltpu.VMEM((row_share, block, tokens), BF16),
            pltpu.VMEM((toks, chips, 16, block), BF16),
            pltpu.VMEM((2, 4, 4, chips // 2, 16, block), BF16),
            pltpu.VMEM((2, 4, chips // 2, 16, block), BF16),
            pltpu.VMEM((2, 4, chips // 2, 16, block), BF16),
            pltpu.VMEM((chips, 16, block), BF16),
            pltpu.VMEM((owners, 16, block), BF16),
            pltpu.VMEM((toks, per_dev // 2, 16, block), BF16),
            pltpu.VMEM((toks, chips, 16, block), BF16),
            pltpu.VMEM((toks, 3 * per_dev // 2, 16, block), BF16),
            pltpu.VMEM((owners + 1, 2, half, block), F32),
            pltpu.VMEM((2, cols, half, block), BF16),
            pltpu.VMEM((cols, half, block), BF16),
            pltpu.VMEM((2, ring + 1) + piece, BF16),
            pltpu.VMEM((2, ring + 1) + piece, BF16),
            pltpu.VMEM((2,) + piece, BF16),
            dma((3,)),
            dma((2, ring + 1)),
            dma((2, ring + 1)),
            dma((2, ring + 1)),
            dma((2, ring + 1)),
            dma((4, chips)),
            dma((4, chips)),
            dma((6,)),
            dma((6,)),
            dma((4, 2, 5, 4)),
            dma((4, 2, 5, 4)),
            dma((2, ring + 1)),
            dma((2, ring + 1)),
        ],
        compiler_params=pltpu.CompilerParams(
            collective_id=0, has_side_effects=True, vmem_limit_bytes=48 * 2**20
        ),
        name="projection_step",
    )(table, cot, hidden, old_weight, old_first, old_second)

    y = y.transpose(0, 2, 1, 3).reshape(tokens, chunk * block)
    output = lax.dynamic_slice_in_dim(y, core * grad_out.shape[1], grad_out.shape[1], 1)
    return (output, new_weight, new_first, new_second)


def solution(mesh):
    state = P("own", None, None)
    in_specs = (P("tok", "own"), P("tok", "own"), state, state, state, P(), P(), P())
    out_specs = (P("tok", "own"), state, state, state)
    return jax.shard_map(local, mesh=mesh, in_specs=in_specs, out_specs=out_specs, check_vma=False)
```

```python
import functools

import jax
import jax.numpy as jnp
from jax import lax
from jax.experimental import pallas as pl
from jax.experimental.pallas import tpu as pltpu
from jax.sharding import PartitionSpec as P

MESH = pl.DeviceIdType.MESH

beta_one = 0.9
beta_two = 0.95
rate = 0.1
epsilon = 0.1
fix_one = 1.0 - 0.9**10
fix_two = 1.0 - 0.95**10

BLOCK = 128
ROWS = 8
F32 = jnp.float32
BF16 = jnp.bfloat16


SEND_SLOT = 0
HOP_OLD, HOP_KEPT = 1, 2
ROW_ROW, ROW_COL = 3, 4
NEW_OLD, NEW_ROW, NEW_KEPT = 5, 6, 7
CELL = 8
TABLE_ROWS = 16


def table_kernel(owners, per_dev, row_share, cols, owner_ref, old_ref, new_ref, table_ref):
    me = lax.axis_index("own")
    total = owner_ref.shape[0]
    shape = (cols, total)

    def spread(row):
        return jnp.broadcast_to(row, shape)

    owner = spread(owner_ref[...].reshape(1, total))
    new_row, new_col = spread(new_ref[0:1, :]), spread(new_ref[1:2, :])
    same = (old_ref[0:1, :] == new_ref[0:1, :]) & (old_ref[1:2, :] == new_ref[1:2, :])
    kept = spread(same.astype(jnp.int32))
    slot = lax.broadcasted_iota(jnp.int32, shape, 0)
    index = lax.broadcasted_iota(jnp.int32, shape, 1)
    row_in = new_row - me * row_share
    row_mine = (row_in >= 0) & (row_in < row_share)
    zero = jnp.zeros(shape, jnp.int32)
    lane = lax.broadcasted_iota(jnp.int32, (cols, 128), 1)
    columns = []

    def pick(where, value):
        return jnp.sum(jnp.where(where, value, zero), axis=1, keepdims=True)

    def put(row, value):
        columns.append((row, value))

    def place(value, share):
        own = jnp.zeros_like(value)
        for i in range(1, owners):
            own += (value >= i * share).astype(jnp.int32)
        return (own & 1) * (owners // 2) + (own >> 1)

    local = index - me * per_dev
    put(SEND_SLOT, pick((owner == slot) & (local >= 0) & (local < per_dev), local))

    mine = owner == me
    row_at = new_row - slot * row_share
    hop = pick(mine & (row_at >= 0) & (row_at < row_share), index * 2 + kept)
    put(HOP_OLD, place(hop >> 1, per_dev))
    put(HOP_KEPT, hop & 1)

    at_row = pick((owner == slot) & row_mine, new_col * 256 + row_in)
    put(ROW_COL, at_row >> 8)
    put(ROW_ROW, at_row & 255)

    down = lax.broadcasted_iota(jnp.int32, (total, total), 0)
    across = lax.broadcasted_iota(jnp.int32, (total, total), 1)
    earlier = jnp.where(down < across, 1.0, 0.0).astype(BF16)
    mine_once = jnp.where(mine[:16], 1.0, 0.0).astype(BF16)
    rank = jnp.dot(mine_once, earlier, preferred_element_type=F32)[0:1, :].astype(jnp.int32)
    at_new = pick(mine & (spread(rank) == slot), (index * 2 + kept) * 256 + new_row)
    put(NEW_OLD, place(at_new >> 9, per_dev))
    put(NEW_ROW, place(at_new & 255, row_share))
    put(NEW_KEPT, (at_new >> 8) & 1)

    for r in range(row_share):
        put(CELL + r, owners + pick((row_in == r) & (new_col == slot), owner - owners))

    turned = jnp.zeros((cols, 128), F32)
    for row, value in columns:
        turned = jnp.where(lane == row, value.astype(F32), turned)
    turned = jnp.concatenate([turned, jnp.zeros((128 - cols, 128), F32)], 0).T
    table_ref[...] = turned[:TABLE_ROWS].astype(jnp.int32)


def adam_update(weight, first, second, grad):
    moment = beta_one * first + (1.0 - beta_one) * grad
    square = beta_two * second + (1.0 - beta_two) * grad * grad
    change = (rate / fix_one) * moment / (jnp.sqrt(square * (1.0 / fix_two)) + epsilon)
    return weight - change, moment, square


JUMP = 5


def step_kernel(
    scale,
    table,
    cot,
    hid,
    old_w,
    old_m,
    old_v,
    out_y,
    out_w,
    out_m,
    out_v,
    loc_w,
    loc_m,
    loc_v,
    w1_out,
    w1_in,
    w2_out,
    w2_in,
    mv_out,
    mv_in,
    cot_all,
    hid_b,
    hid_t,
    g_out,
    g_one,
    g_mid,
    g_two,
    g_sum,
    g_new,
    g_all,
    w_all,
    state,
    prod,
    part,
    part_sib,
    rs_out,
    rs_in,
    fin,
    loc_sem,
    cot_send,
    cot_recv,
    sib_send,
    sib_recv,
    z_send,
    z_recv,
    fwd_send,
    fwd_recv,
    xy_send,
    xy_recv,
    rs_send,
    rs_recv,
):
    toks, owners = lax.axis_size("tok"), lax.axis_size("own")
    side = 4
    chips = owners // 2
    t, o = lax.axis_index("tok"), lax.axis_index("own")
    z, core = o // 2, o % 2
    y, x = t // side, t % side
    sibling = {"tok": t, "own": z * 2 + 1 - core}
    per_dev = old_w.shape[0]
    half_dev = per_dev // 2
    row_share = hid_t.shape[0]
    cols = part.shape[1]
    units = cot.shape[0] // (BLOCK // 2)
    chunk = cols // chips
    half = BLOCK // 2
    pairs = owners // 2
    reach = (chips // 2, chips - 1 - chips // 2)

    def remote(src, dst, send, recv, device):
        return pltpu.make_async_remote_copy(
            src_ref=src, dst_ref=dst, send_sem=send, recv_sem=recv, device_id=device, device_id_type=MESH
        )

    def along_z(d):
        return {"tok": t, "own": ((z + d) % chips) * 2 + core}

    def tok_at(dy, dx):
        return ((y + dy) % side) * side + (x + dx) % side

    def across(dy, dx):
        return {"tok": tok_at(dy, dx), "own": o}

    def loop(first, last, body):
        def step(i, carry):
            body(i)
            return carry

        lax.fori_loop(first, last, step, 0)

    loc = (loc_w, loc_m, loc_v)

    def loop_by(n, last, body):
        def several(i):
            for j in range(n):
                body(i * n + j)

        loop(0, last // n, several)

    rows = pl.ds((t // 2) * 16, 16)
    local = [
        pltpu.make_async_copy(old.at[:, rows, :], loc[i], loc_sem.at[i])
        for i, old in enumerate((old_w, old_m, old_v))
    ]
    for copy in local:
        copy.start()
    barrier = pltpu.get_barrier_semaphore()

    def greet(device):
        pl.semaphore_signal(barrier, inc=1, device_id=device, device_id_type=MESH)

    greet(sibling)
    loop(1, chips, lambda d: greet(along_z(d)))
    loop(1, side, lambda d: greet(across(0, d)))
    loop(1, side, lambda d: greet(across(d, 0)))

    def is_one(bit):
        return (jnp.zeros((ROWS, BLOCK), jnp.int32) + bit) == 1

    odd_rows, second_core = is_one(t % 2), is_one(core)

    def own_rows(i, k):
        both = loc[i][k].astype(F32)
        return jnp.where(odd_rows, both[ROWS:], both[:ROWS])

    def core_rows(tile):
        both = tile.astype(F32)
        return jnp.where(second_core, both[ROWS:], both[:ROWS])

    def stack(a, b):
        return jnp.concatenate([a, b], 0).astype(BF16)

    for i in range(units):
        cot_all[o * units + i] = cot[i * half : (i + 1) * half, :]
    local[0].wait()

    def pack_w1(k):
        w1_out[k] = stack(own_rows(0, table[SEND_SLOT, 2 * k]), own_rows(0, table[SEND_SLOT, 2 * k + 1]))

    loop_by(4, chips, pack_w1)
    pl.semaphore_wait(barrier, chips - 1 + 1 + 2 * (side - 1))

    def cot_at(way, distance):
        zz = z + chips - distance if way == 0 else z + distance
        own = (zz % chips) * 2 + core
        return cot_all.at[pl.ds(own * units, units)]

    def cot_hop(way, distance):
        step = distance if distance in (1, JUMP) else 1
        ref = cot_at(way, distance - step)
        return remote(
            ref,
            ref,
            cot_send.at[way, distance],
            cot_recv.at[way, distance],
            along_z(step if way == 0 else chips - step),
        )

    def cot_aside(way, distance):
        ref = cot_at(way, distance)
        return remote(ref, ref, sib_send.at[way, distance], sib_recv.at[way, distance], sibling)

    def cot_step(distance):
        for way in range(2):
            if distance <= reach[way]:
                cot_hop(way, distance).wait_recv()
                if distance + 1 <= reach[way] and distance + 1 != JUMP:
                    cot_hop(way, distance + 1).start()
                cot_aside(way, distance).start()

    def far_first(i):
        return chips // 2 + ((i + 1) // 2) * (1 - 2 * (i % 2))

    def z_copy(plane, src, dst, d):
        zz = (z + d) % chips
        return remote(
            src(zz),
            dst.at[core * chips + z],
            z_send.at[plane, d],
            z_recv.at[plane, d],
            {"tok": t, "own": zz * 2 + core},
        )

    def forward(plane, ref):
        return remote(ref, ref, fwd_send.at[plane], fwd_recv.at[plane], sibling)

    my_chips = pl.ds(core * chips, chips)
    z_all = {
        "w1": (0, lambda zz: w1_out.at[zz], w1_in),
        "mv": (1, lambda zz: mv_out.at[pl.ds(2 * zz, 2)], mv_in),
        "w2": (2, lambda zz: w2_out.at[zz], w2_in),
        "g": (3, lambda zz: g_sum.at[zz], g_new),
    }
    fwd = {
        "w1": forward(0, w1_in.at[my_chips]),
        "mv": forward(1, mv_in.at[my_chips, 1 - core]),
        "w2": forward(2, w2_in.at[my_chips]),
        "g": forward(3, g_new.at[my_chips]),
    }

    def z_start(name):
        loop(0, chips - 1, lambda i: z_copy(*z_all[name], far_first(i)).start())

    def z_wait(name):
        loop(1, chips, lambda d: z_copy(*z_all[name], d).wait_recv())
        fwd[name].start()

    def xy_one(plane, at, h, d):
        ref = at(h, t)
        to = across(0, d) if h == 0 else across(d, 0)
        return remote(ref, ref, xy_send.at[plane, h, 0, d], xy_recv.at[plane, h, 0, d], to)

    def xy_two(plane, at, h, e, d):
        ref = at(h, tok_at(0, e) if h == 0 else tok_at(e, 0))
        to = across(d, 0) if h == 0 else across(0, d)
        return remote(ref, ref, xy_send.at[plane, h, 1 + e, d], xy_recv.at[plane, h, 1 + e, d], to)

    def ag_start(plane, at):
        for h in range(2):
            loop(1, side, lambda d: xy_one(plane, at, h, d).start())
        for h in range(2):
            loop(1, side, lambda d: xy_two(plane, at, h, 0, d).start())

    def ag_pass_on(plane, at):
        def pass_on(d):
            for h in range(2):
                xy_one(plane, at, h, d).wait_recv()
                loop(1, side, lambda dd: xy_two(plane, at, h, side - d, dd).start())

        loop(1, side, pass_on)

    def ag_each(plane, at, do):
        for h in range(2):
            loop(0, side, lambda e: loop(1, side, lambda d: do(xy_two(plane, at, h, e, d))))

    def ag_wait(plane, at):
        ag_each(plane, at, lambda copy: copy.wait_recv())

    def ag_sent(plane, at):
        for h in range(2):
            loop(1, side, lambda d: xy_one(plane, at, h, d).wait_send())
        ag_each(plane, at, lambda copy: copy.wait_send())

    def halves(ref):
        n = ref.shape[1] // 2
        return lambda h, i: ref.at[i, pl.ds(h * n, n)]

    ag_w, ag_state, ag_g = (0, halves(w_all)), (1, halves(state)), (2, halves(g_all))

    def cot_begin():
        for way in range(2):
            cot_hop(way, 1).start()
        for way in range(2):
            if JUMP <= reach[way]:
                cot_hop(way, JUMP).start()
        cot_aside(0, 0).start()

    def cot_end():
        cot_aside(0, 0).wait_recv()
        for way in range(2):
            for distance in range(1, reach[way] + 1):
                cot_aside(way, distance).wait_recv()

    def w1_begin():
        z_start("w1")
        w1_in[core * chips + z] = w1_out[z]

    def lay_mv():
        for i in (1, 2):
            local[i].wait()

        def pack_mv(n):
            k = table[SEND_SLOT, n]
            mv_out[n] = stack(own_rows(1, k), own_rows(2, k))

        loop_by(4, owners, pack_mv)
        mv_in[core * chips + z] = mv_out[pl.ds(2 * z, 2)]

    def lay_hid():
        for r in range(row_share):
            block = hid[:, r * BLOCK : (r + 1) * BLOCK]
            hid_b[r] = block
            hid_t[r] = block.astype(F32).T.astype(BF16)
        prod[owners] = jnp.zeros(prod.shape[1:], F32)

    def w2_begin():
        def pack_w2(k):
            parts = []
            for r in (2 * k, 2 * k + 1):
                parts.append(core_rows(w1_in[table[HOP_OLD, r]]) * table[HOP_KEPT, r].astype(F32))
            w2_out[k] = stack(*parts)

        loop_by(4, chips, pack_w2)
        z_start("w2")
        w2_in[core * chips + z] = w2_out[z]

    def grad_pair(k):
        slices = []
        for n in (2 * k, 2 * k + 1):
            at = table[ROW_COL, n] * 2
            cot_t = jnp.concatenate([cot_all[at], cot_all[at + 1]], 0)
            g = lax.dot_general(
                hid_t[table[ROW_ROW, n]], cot_t, (((1,), (1,)), ((), ())), preferred_element_type=F32
            )
            slices.append((g * scale).reshape(toks, ROWS, BLOCK))
        g_out[:, k] = jnp.concatenate(slices, 1).astype(BF16)

    def half_pairs(h):
        return pl.ds(h * (pairs // 2), pairs // 2)

    def g_first(h, e, d):
        to = tok_at(e, d) if h == 0 else tok_at(d, e)
        return remote(
            g_out.at[to, half_pairs(h)],
            g_one.at[h, d, e],
            xy_send.at[3, h, 1 + e, d],
            xy_recv.at[3, h, 1 + e, d],
            across(0, d) if h == 0 else across(d, 0),
        )

    def g_second(h, e):
        return remote(
            g_mid.at[h, e],
            g_two.at[h, e],
            xy_send.at[3, h, 0, e],
            xy_recv.at[3, h, 0, e],
            across(e, 0) if h == 0 else across(0, e),
        )

    def g_each(do):
        for h in range(2):
            loop(1, side, lambda e: loop(1, side, lambda d: do(g_first(h, e, d))))
        for h in range(2):
            loop(1, side, lambda d: do(g_first(h, 0, d)))

    def g_begin():
        loop_by(4, pairs, grad_pair)
        g_each(lambda copy: copy.start())

    def w_begin():
        def pack_w(k):
            w_all[t, k] = stack(core_rows(w2_in[k]), core_rows(w2_in[chips + k]))

        loop_by(4, pairs, pack_w)
        ag_start(*ag_w)

    def g_middle(e):
        for h in range(2):
            loop(1, side, lambda d: g_first(h, e, d).wait_recv())
            own = g_out[tok_at(e, 0) if h == 0 else tok_at(0, e), half_pairs(h)].astype(F32)
            others = [g_one[h, d, e].astype(F32) for d in range(1, side)]
            g_mid[h, e] = (own + others[0] + others[1] + others[2]).astype(BF16)

    def g_on(e):
        g_middle(e)
        for h in range(2):
            g_second(h, e).start()

    def g_pass_on():
        loop(1, side, g_on)

    def gz_begin():
        g_middle(0)
        for h in range(2):
            loop(1, side, lambda e: g_second(h, e).wait_recv())
            total = g_mid[h, 0].astype(F32)
            for e in range(1, side):
                total += g_two[h, e].astype(F32)
            g_sum[half_pairs(h)] = total.astype(BF16)
        z_start("g")
        g_new[core * chips + z] = g_sum[z]

    def state_begin():
        def pack_state(p):
            parts = []
            for s in (2 * p, 2 * p + 1):
                kept = table[NEW_KEPT, s].astype(F32)
                place = table[NEW_OLD, s]
                both = mv_in[place, core].astype(F32) * kept
                parts.append((core_rows(w1_in[place]) * kept, both[:ROWS], both[ROWS:]))
            for i in range(3):
                state[t, i * half_dev + p] = stack(parts[0][i], parts[1][i])

        loop_by(4, half_dev, pack_state)
        ag_start(*ag_state)

    def product(k):
        both = w_all[:, k].astype(F32)
        for i in range(2):
            n = 2 * k + i
            w = both[:, i * ROWS : (i + 1) * ROWS].reshape(BLOCK, BLOCK).astype(BF16)
            p = jnp.dot(hid_b[table[ROW_ROW, n]], w, preferred_element_type=F32) * scale
            prod[n] = p.reshape(2, half, BLOCK)

    def gather_part(h):
        def column(c):
            total = prod[table[CELL, c], h]
            for r in range(1, row_share):
                total += prod[table[CELL + r, c], h]
            part[h, c] = total.astype(BF16)

        loop_by(4, cols, column)

    swap = remote(part.at[1 - core], part_sib, fwd_send.at[4], fwd_recv.at[4], sibling)

    def part_begin():
        loop_by(4, pairs, product)
        gather_part(1 - core)
        swap.start()

    def term(zz):
        at = pl.ds((zz % chips) * chunk, chunk)
        return part[core, at].astype(F32) + part_sib[at].astype(F32)

    def rs_hop(way, distance):
        step = JUMP if distance == JUMP else 1
        return remote(
            rs_out.at[way, distance],
            rs_in.at[way, distance],
            rs_send.at[way, distance],
            rs_recv.at[way, distance],
            along_z(step if way == 0 else chips - step),
        )

    def rs_step(way, distance):
        if distance > reach[way]:
            return
        value = term(z + distance if way == 0 else z + chips - distance)
        if distance not in (JUMP - 1, reach[way]):
            rs_hop(way, distance + 1).wait_recv()
            value += rs_in[way, distance + 1].astype(F32)
        rs_out[way, distance] = value.astype(BF16)
        rs_hop(way, distance).start()

    def rs_round(k):
        for way in range(2):
            if reach[way] - k >= JUMP:
                rs_step(way, reach[way] - k)
        for way in range(2):
            if JUMP - 1 - k >= 1:
                rs_step(way, min(JUMP - 1, reach[way]) - k)

    finish = remote(fin.at[core], fin.at[core], fwd_send.at[5], fwd_recv.at[5], sibling)

    def rs_end():
        value = term(z)
        for way in range(2):
            for distance in (1, JUMP):
                if distance <= reach[way]:
                    rs_hop(way, distance).wait_recv()
                    value += rs_in[way, distance].astype(F32)
        fin[core] = value.astype(BF16)
        finish.start()

    def ga_begin():
        def pack_g(p):
            g_all[t, p] = stack(*[core_rows(g_new[table[NEW_ROW, s]]) for s in (2 * p, 2 * p + 1)])

        loop_by(4, half_dev, pack_g)
        ag_start(*ag_g)

    def adam(p):
        g, w, m, v = [
            ref[:, i].astype(F32)
            for ref, i in ((g_all, p), (state, p), (state, half_dev + p), (state, 2 * half_dev + p))
        ]
        for result, value in zip((out_w, out_m, out_v), adam_update(w, m, v, g)):
            for i in range(2):
                part_rows = value[:, i * ROWS : (i + 1) * ROWS]
                result[2 * p + i] = part_rows.reshape(BLOCK, BLOCK).astype(BF16)

    cot_begin()
    w1_begin()
    lay_mv()
    lay_hid()
    cot_step(1)
    z_wait("w1")
    cot_step(5)
    fwd["w1"].wait_recv()
    w2_begin()
    for distance in (2, 6, 3, 7):
        cot_step(distance)
    z_wait("w2")
    cot_step(4)
    fwd["w2"].wait_recv()
    w_begin()
    cot_step(8)
    z_start("mv")
    ag_pass_on(*ag_w)
    cot_end()
    g_begin()
    g_pass_on()
    z_wait("mv")
    ag_wait(*ag_w)
    part_begin()
    gather_part(core)
    gz_begin()
    fwd["mv"].wait_recv()
    state_begin()
    swap.wait_recv()
    rs_round(0)
    ag_pass_on(*ag_state)
    rs_round(1)
    z_wait("g")
    rs_round(2)
    fwd["g"].wait_recv()
    ga_begin()
    rs_round(3)
    ag_pass_on(*ag_g)
    rs_end()
    ag_wait(*ag_state)
    ag_wait(*ag_g)
    loop_by(2, half_dev, adam)
    finish.wait_recv()
    out_y[...] = fin[...]

    cot_aside(0, 0).wait_send()
    for way in range(2):
        for distance in range(1, reach[way] + 1):
            cot_hop(way, distance).wait_send()
            cot_aside(way, distance).wait_send()
            rs_hop(way, distance).wait_send()
    for name in z_all:
        loop(1, chips, lambda d: z_copy(*z_all[name], d).wait_send())
        fwd[name].wait_send()
    for gather in (ag_w, ag_state, ag_g):
        ag_sent(*gather)
    g_each(lambda copy: copy.wait_send())
    for h in range(2):
        loop(1, side, lambda e: g_second(h, e).wait_send())
    swap.wait_send()
    finish.wait_send()


def local(hidden, grad_out, old_weight, old_first, old_second, old_blocks, new_blocks, new_owner):
    owners, toks = lax.axis_size("own"), lax.axis_size("tok")
    chips = owners // 2
    core = lax.axis_index("own") % 2
    per_dev, block = old_weight.shape[0], old_weight.shape[1]
    total = new_owner.shape[0]
    tokens = hidden.shape[0]
    row_share = hidden.shape[1] // block
    width = grad_out.shape[1] * owners
    cols = width // block
    chunk = cols // chips
    half = block // 2
    scale = (total * block * block / width) ** (-0.5)

    vmem = pl.BlockSpec(memory_space=pltpu.VMEM)
    hbm = pl.BlockSpec(memory_space=pltpu.HBM)
    table = pl.pallas_call(
        functools.partial(table_kernel, owners, per_dev, row_share, cols),
        out_shape=jax.ShapeDtypeStruct((TABLE_ROWS, 128), jnp.int32),
        in_specs=[vmem, vmem, vmem],
        out_specs=vmem,
        compiler_params=pltpu.CompilerParams(vmem_limit_bytes=32 * 2**20),
        name="block_table",
    )(new_owner, old_blocks.T, new_blocks.T)

    dma = pltpu.SemaphoreType.DMA
    ring = chips // 2
    piece = (chunk, half, block)
    state_shape = jax.ShapeDtypeStruct(old_weight.shape, BF16)
    y, new_weight, new_first, new_second = pl.pallas_call(
        functools.partial(step_kernel, scale),
        out_shape=(jax.ShapeDtypeStruct((2,) + piece, BF16), state_shape, state_shape, state_shape),
        in_specs=[pl.BlockSpec(memory_space=pltpu.SMEM), vmem, vmem, hbm, hbm, hbm],
        out_specs=(vmem, vmem, vmem, vmem),
        scratch_shapes=[
            pltpu.VMEM((per_dev, 16, block), BF16),
            pltpu.VMEM((per_dev, 16, block), BF16),
            pltpu.VMEM((per_dev, 16, block), BF16),
            pltpu.VMEM((chips, 16, block), BF16),
            pltpu.VMEM((owners, 16, block), BF16),
            pltpu.VMEM((chips, 16, block), BF16),
            pltpu.VMEM((owners, 16, block), BF16),
            pltpu.VMEM((owners, 16, block), BF16),
            pltpu.VMEM((owners, 2, 16, block), BF16),
            pltpu.VMEM((2 * cols, half, tokens), BF16),
            pltpu.VMEM((row_share, tokens, block), BF16),
            pltpu.VMEM((row_share, block, tokens), BF16),
            pltpu.VMEM((toks, chips, 16, block), BF16),
            pltpu.VMEM((2, 4, 4, chips // 2, 16, block), BF16),
            pltpu.VMEM((2, 4, chips // 2, 16, block), BF16),
            pltpu.VMEM((2, 4, chips // 2, 16, block), BF16),
            pltpu.VMEM((chips, 16, block), BF16),
            pltpu.VMEM((owners, 16, block), BF16),
            pltpu.VMEM((toks, per_dev // 2, 16, block), BF16),
            pltpu.VMEM((toks, chips, 16, block), BF16),
            pltpu.VMEM((toks, 3 * per_dev // 2, 16, block), BF16),
            pltpu.VMEM((owners + 1, 2, half, block), F32),
            pltpu.VMEM((2, cols, half, block), BF16),
            pltpu.VMEM((cols, half, block), BF16),
            pltpu.VMEM((2, ring + 1) + piece, BF16),
            pltpu.VMEM((2, ring + 1) + piece, BF16),
            pltpu.VMEM((2,) + piece, BF16),
            dma((3,)),
            dma((2, ring + 1)),
            dma((2, ring + 1)),
            dma((2, ring + 1)),
            dma((2, ring + 1)),
            dma((4, chips)),
            dma((4, chips)),
            dma((6,)),
            dma((6,)),
            dma((4, 2, 5, 4)),
            dma((4, 2, 5, 4)),
            dma((2, ring + 1)),
            dma((2, ring + 1)),
        ],
        compiler_params=pltpu.CompilerParams(
            collective_id=0, has_side_effects=True, vmem_limit_bytes=60 * 2**20
        ),
        name="projection_step",
    )(table, grad_out.T, hidden, old_weight, old_first, old_second)

    y = y.transpose(0, 2, 1, 3).reshape(tokens, chunk * block)
    output = lax.dynamic_slice_in_dim(y, core * grad_out.shape[1], grad_out.shape[1], 1)
    return (output, new_weight, new_first, new_second)


def solution(mesh):
    state = P("own", None, None)
    in_specs = (P("tok", "own"), P("tok", "own"), state, state, state, P(), P(), P())
    out_specs = (P("tok", "own"), state, state, state)
    return jax.shard_map(local, mesh=mesh, in_specs=in_specs, out_specs=out_specs, check_vma=False)
```

```python
import functools

import jax
import jax.numpy as jnp
from jax import lax
from jax.experimental import pallas as pl
from jax.experimental.pallas import tpu as pltpu
from jax.sharding import PartitionSpec as P

MESH = pl.DeviceIdType.MESH

beta_one = 0.9
beta_two = 0.95
rate = 0.1
epsilon = 0.1
fix_one = 1.0 - 0.9**10
fix_two = 1.0 - 0.95**10

BLOCK = 128
ROWS = 8
F32 = jnp.float32
BF16 = jnp.bfloat16


SEND_SLOT = 0
HOP_OLD, HOP_KEPT = 1, 2
ROW_ROW, ROW_COL = 3, 4
NEW_OLD, NEW_ROW, NEW_KEPT = 5, 6, 7
CELL = 8
TABLE_ROWS = 16


def table_kernel(owners, per_dev, row_share, cols, owner_ref, old_ref, new_ref, *refs):
    olds, table_ref, mine_refs, sem = refs[:3], refs[3], refs[4:7], refs[7]
    rows = pl.ds((lax.axis_index("tok") // 2) * 16, 16)
    copies = [
        pltpu.make_async_copy(old.at[:, rows, :], ref, sem.at[i]) for i, (old, ref) in enumerate(zip(olds, mine_refs))
    ]
    for copy in copies:
        copy.start()
    me = lax.axis_index("own")
    total = owner_ref.shape[0]
    shape = (cols, total)

    def spread(row):
        return jnp.broadcast_to(row, shape)

    owner = spread(owner_ref[...].reshape(1, total))
    new_row, new_col = spread(new_ref[0:1, :]), spread(new_ref[1:2, :])
    same = (old_ref[0:1, :] == new_ref[0:1, :]) & (old_ref[1:2, :] == new_ref[1:2, :])
    kept = spread(same.astype(jnp.int32))
    slot = lax.broadcasted_iota(jnp.int32, shape, 0)
    index = lax.broadcasted_iota(jnp.int32, shape, 1)
    row_in = new_row - me * row_share
    row_mine = (row_in >= 0) & (row_in < row_share)
    zero = jnp.zeros(shape, jnp.int32)
    lane = lax.broadcasted_iota(jnp.int32, (cols, 128), 1)
    columns = []

    def pick(where, value):
        return jnp.sum(jnp.where(where, value, zero), axis=1, keepdims=True)

    def put(row, value):
        columns.append((row, value))

    def place(value, share):
        own = jnp.zeros_like(value)
        for i in range(1, owners):
            own += (value >= i * share).astype(jnp.int32)
        return (own & 1) * (owners // 2) + (own >> 1)

    local = index - me * per_dev
    put(SEND_SLOT, pick((owner == slot) & (local >= 0) & (local < per_dev), local))

    mine = owner == me
    row_at = new_row - slot * row_share
    hop = pick(mine & (row_at >= 0) & (row_at < row_share), index * 2 + kept)
    put(HOP_OLD, place(hop >> 1, per_dev))
    put(HOP_KEPT, hop & 1)

    at_row = pick((owner == slot) & row_mine, new_col * 256 + row_in)
    put(ROW_COL, at_row >> 8)
    put(ROW_ROW, at_row & 255)

    down = lax.broadcasted_iota(jnp.int32, (total, total), 0)
    across = lax.broadcasted_iota(jnp.int32, (total, total), 1)
    earlier = jnp.where(down < across, 1.0, 0.0).astype(BF16)
    mine_once = jnp.where(mine[:16], 1.0, 0.0).astype(BF16)
    rank = jnp.dot(mine_once, earlier, preferred_element_type=F32)[0:1, :].astype(jnp.int32)
    at_new = pick(mine & (spread(rank) == slot), (index * 2 + kept) * 256 + new_row)
    put(NEW_OLD, place(at_new >> 9, per_dev))
    put(NEW_ROW, place(at_new & 255, row_share))
    put(NEW_KEPT, (at_new >> 8) & 1)

    for r in range(row_share):
        put(CELL + r, owners + pick((row_in == r) & (new_col == slot), owner - owners))

    turned = jnp.zeros((cols, 128), F32)
    for row, value in columns:
        turned = jnp.where(lane == row, value.astype(F32), turned)
    turned = jnp.concatenate([turned, jnp.zeros((128 - cols, 128), F32)], 0).T
    table_ref[...] = turned[:TABLE_ROWS].astype(jnp.int32)
    for copy in copies:
        copy.wait()


def adam_update(weight, first, second, grad):
    moment = beta_one * first + (1.0 - beta_one) * grad
    square = beta_two * second + (1.0 - beta_two) * grad * grad
    change = (rate / fix_one) * moment / (jnp.sqrt(square * (1.0 / fix_two)) + epsilon)
    return weight - change, moment, square


TABLE_VMEM = 53
STEP_VMEM = 48
JUMP = 5


def step_kernel(
    scale,
    table,
    cot,
    hid,
    loc_w,
    loc_m,
    loc_v,
    fin,
    g_all,
    state,
    w1_out,
    w1_in,
    w2_out,
    w2_in,
    mv_out,
    mv_in,
    cot_all,
    hid_b,
    hid_t,
    g_out,
    g_one,
    g_mid,
    g_two,
    g_sum,
    g_new,
    w_all,
    prod,
    part,
    part_sib,
    rs_out,
    rs_in,
    cot_send,
    cot_recv,
    sib_send,
    sib_recv,
    z_send,
    z_recv,
    fwd_send,
    fwd_recv,
    xy_send,
    xy_recv,
    rs_send,
    rs_recv,
):
    toks, owners = lax.axis_size("tok"), lax.axis_size("own")
    side = 4
    chips = owners // 2
    t, o = lax.axis_index("tok"), lax.axis_index("own")
    z, core = o // 2, o % 2
    y, x = t // side, t % side
    sibling = {"tok": t, "own": z * 2 + 1 - core}
    per_dev = loc_w.shape[0]
    half_dev = per_dev // 2
    row_share = hid_t.shape[0]
    cols = part.shape[1]
    units = cot.shape[0] // (BLOCK // 2)
    chunk = cols // chips
    half = BLOCK // 2
    pairs = owners // 2
    reach = (chips // 2, chips - 1 - chips // 2)

    def remote(src, dst, send, recv, device):
        return pltpu.make_async_remote_copy(
            src_ref=src, dst_ref=dst, send_sem=send, recv_sem=recv, device_id=device, device_id_type=MESH
        )

    def along_z(d):
        return {"tok": t, "own": ((z + d) % chips) * 2 + core}

    def tok_at(dy, dx):
        return ((y + dy) % side) * side + (x + dx) % side

    def across(dy, dx):
        return {"tok": tok_at(dy, dx), "own": o}

    def loop(first, last, body):
        def step(i, carry):
            body(i)
            return carry

        lax.fori_loop(first, last, step, 0)

    loc = (loc_w, loc_m, loc_v)

    def loop_by(n, last, body):
        def several(i):
            for j in range(n):
                body(i * n + j)

        loop(0, last // n, several)

    barrier = pltpu.get_barrier_semaphore()

    def greet(device):
        pl.semaphore_signal(barrier, inc=1, device_id=device, device_id_type=MESH)

    greet(sibling)
    loop(1, chips, lambda d: greet(along_z(d)))
    loop(1, side, lambda d: greet(across(0, d)))
    loop(1, side, lambda d: greet(across(d, 0)))

    def is_one(bit):
        return (jnp.zeros((ROWS, BLOCK), jnp.int32) + bit) == 1

    odd_rows, second_core = is_one(t % 2), is_one(core)

    def own_rows(i, k):
        both = loc[i][k].astype(F32)
        return jnp.where(odd_rows, both[ROWS:], both[:ROWS])

    def core_rows(tile):
        both = tile.astype(F32)
        return jnp.where(second_core, both[ROWS:], both[:ROWS])

    def stack(a, b):
        return jnp.concatenate([a, b], 0).astype(BF16)

    for i in range(units):
        cot_all[o * units + i] = cot[i * half : (i + 1) * half, :]

    def pack_w1(k):
        w1_out[k] = stack(own_rows(0, table[SEND_SLOT, 2 * k]), own_rows(0, table[SEND_SLOT, 2 * k + 1]))

    loop_by(4, chips, pack_w1)
    pl.semaphore_wait(barrier, chips - 1 + 1 + 2 * (side - 1))

    def cot_at(way, distance):
        zz = z + chips - distance if way == 0 else z + distance
        own = (zz % chips) * 2 + core
        return cot_all.at[pl.ds(own * units, units)]

    def cot_hop(way, distance):
        step = distance if distance in (1, JUMP) else 1
        ref = cot_at(way, distance - step)
        return remote(
            ref,
            ref,
            cot_send.at[way, distance],
            cot_recv.at[way, distance],
            along_z(step if way == 0 else chips - step),
        )

    def cot_aside(way, distance):
        ref = cot_at(way, distance)
        return remote(ref, ref, sib_send.at[way, distance], sib_recv.at[way, distance], sibling)

    def cot_step(distance):
        for way in range(2):
            if distance <= reach[way]:
                cot_hop(way, distance).wait_recv()
                if distance + 1 <= reach[way] and distance + 1 != JUMP:
                    cot_hop(way, distance + 1).start()
                cot_aside(way, distance).start()

    def far_first(i):
        return chips // 2 + ((i + 1) // 2) * (1 - 2 * (i % 2))

    def z_copy(plane, src, dst, d):
        zz = (z + d) % chips
        return remote(
            src(zz),
            dst.at[core * chips + z],
            z_send.at[plane, d],
            z_recv.at[plane, d],
            {"tok": t, "own": zz * 2 + core},
        )

    def forward(plane, ref):
        return remote(ref, ref, fwd_send.at[plane], fwd_recv.at[plane], sibling)

    my_chips = pl.ds(core * chips, chips)
    z_all = {
        "w1": (0, lambda zz: w1_out.at[zz], w1_in),
        "mv": (1, lambda zz: mv_out.at[pl.ds(2 * zz, 2)], mv_in),
        "w2": (2, lambda zz: w2_out.at[zz], w2_in),
        "g": (3, lambda zz: g_sum.at[zz], g_new),
    }
    fwd = {
        "w1": forward(0, w1_in.at[my_chips]),
        "mv": forward(1, mv_in.at[my_chips, 1 - core]),
        "w2": forward(2, w2_in.at[my_chips]),
        "g": forward(3, g_new.at[my_chips]),
    }

    def z_start(name):
        loop(0, chips - 1, lambda i: z_copy(*z_all[name], far_first(i)).start())

    def z_wait(name):
        loop(1, chips, lambda d: z_copy(*z_all[name], d).wait_recv())
        fwd[name].start()

    def xy_one(plane, at, h, d):
        ref = at(h, t)
        to = across(0, d) if h == 0 else across(d, 0)
        return remote(ref, ref, xy_send.at[plane, h, 0, d], xy_recv.at[plane, h, 0, d], to)

    def xy_two(plane, at, h, e, d):
        ref = at(h, tok_at(0, e) if h == 0 else tok_at(e, 0))
        to = across(d, 0) if h == 0 else across(0, d)
        return remote(ref, ref, xy_send.at[plane, h, 1 + e, d], xy_recv.at[plane, h, 1 + e, d], to)

    def ag_start(plane, at):
        for h in range(2):
            loop(1, side, lambda d: xy_one(plane, at, h, d).start())
        for h in range(2):
            loop(1, side, lambda d: xy_two(plane, at, h, 0, d).start())

    def ag_pass_on(plane, at):
        def pass_on(d):
            for h in range(2):
                xy_one(plane, at, h, d).wait_recv()
                loop(1, side, lambda dd: xy_two(plane, at, h, side - d, dd).start())

        loop(1, side, pass_on)

    def ag_each(plane, at, do):
        for h in range(2):
            loop(0, side, lambda e: loop(1, side, lambda d: do(xy_two(plane, at, h, e, d))))

    def ag_wait(plane, at):
        ag_each(plane, at, lambda copy: copy.wait_recv())

    def ag_sent(plane, at):
        for h in range(2):
            loop(1, side, lambda d: xy_one(plane, at, h, d).wait_send())
        ag_each(plane, at, lambda copy: copy.wait_send())

    def halves(ref):
        n = ref.shape[1] // 2
        return lambda h, i: ref.at[i, pl.ds(h * n, n)]

    ag_w, ag_state, ag_g = (0, halves(w_all)), (1, halves(state)), (2, halves(g_all))

    def cot_begin():
        for way in range(2):
            cot_hop(way, 1).start()
        for way in range(2):
            if JUMP <= reach[way]:
                cot_hop(way, JUMP).start()
        cot_aside(0, 0).start()

    def cot_end():
        cot_aside(0, 0).wait_recv()
        for way in range(2):
            for distance in range(1, reach[way] + 1):
                cot_aside(way, distance).wait_recv()

    def w1_begin():
        z_start("w1")
        w1_in[core * chips + z] = w1_out[z]

    def lay_mv():
        def pack_mv(n):
            k = table[SEND_SLOT, n]
            mv_out[n] = stack(own_rows(1, k), own_rows(2, k))

        loop_by(4, owners, pack_mv)
        mv_in[core * chips + z] = mv_out[pl.ds(2 * z, 2)]

    def lay_hid():
        for r in range(row_share):
            block = hid[:, r * BLOCK : (r + 1) * BLOCK]
            hid_b[r] = block
            hid_t[r] = block.astype(F32).T.astype(BF16)
        prod[owners] = jnp.zeros(prod.shape[1:], F32)

    def w2_begin():
        def pack_w2(k):
            parts = []
            for r in (2 * k, 2 * k + 1):
                parts.append(core_rows(w1_in[table[HOP_OLD, r]]) * table[HOP_KEPT, r].astype(F32))
            w2_out[k] = stack(*parts)

        loop_by(4, chips, pack_w2)
        z_start("w2")
        w2_in[core * chips + z] = w2_out[z]

    def grad_pair(k):
        slices = []
        for n in (2 * k, 2 * k + 1):
            at = table[ROW_COL, n] * 2
            cot_t = jnp.concatenate([cot_all[at], cot_all[at + 1]], 0)
            g = lax.dot_general(
                hid_t[table[ROW_ROW, n]], cot_t, (((1,), (1,)), ((), ())), preferred_element_type=F32
            )
            slices.append((g * scale).reshape(toks, ROWS, BLOCK))
        g_out[:, k] = jnp.concatenate(slices, 1).astype(BF16)

    def half_pairs(h):
        return pl.ds(h * (pairs // 2), pairs // 2)

    def g_first(h, e, d):
        to = tok_at(e, d) if h == 0 else tok_at(d, e)
        return remote(
            g_out.at[to, half_pairs(h)],
            g_one.at[h, d, e],
            xy_send.at[3, h, 1 + e, d],
            xy_recv.at[3, h, 1 + e, d],
            across(0, d) if h == 0 else across(d, 0),
        )

    def g_second(h, e):
        return remote(
            g_mid.at[h, e],
            g_two.at[h, e],
            xy_send.at[3, h, 0, e],
            xy_recv.at[3, h, 0, e],
            across(e, 0) if h == 0 else across(0, e),
        )

    def g_each(do):
        for h in range(2):
            loop(1, side, lambda e: loop(1, side, lambda d: do(g_first(h, e, d))))
        for h in range(2):
            loop(1, side, lambda d: do(g_first(h, 0, d)))

    def g_begin():
        loop_by(8, pairs, grad_pair)
        g_each(lambda copy: copy.start())

    def w_begin():
        def pack_w(k):
            w_all[t, k] = stack(core_rows(w2_in[k]), core_rows(w2_in[chips + k]))

        loop_by(4, pairs, pack_w)
        ag_start(*ag_w)

    def g_middle(e):
        for h in range(2):
            loop(1, side, lambda d: g_first(h, e, d).wait_recv())
            own = g_out[tok_at(e, 0) if h == 0 else tok_at(0, e), half_pairs(h)].astype(F32)
            others = [g_one[h, d, e].astype(F32) for d in range(1, side)]
            g_mid[h, e] = (own + others[0] + others[1] + others[2]).astype(BF16)

    def g_on(e):
        g_middle(e)
        for h in range(2):
            g_second(h, e).start()

    def g_pass_on():
        loop(1, side, g_on)

    def gz_begin():
        g_middle(0)
        for h in range(2):
            loop(1, side, lambda e: g_second(h, e).wait_recv())
            total = g_mid[h, 0].astype(F32)
            for e in range(1, side):
                total += g_two[h, e].astype(F32)
            g_sum[half_pairs(h)] = total.astype(BF16)
        z_start("g")
        g_new[core * chips + z] = g_sum[z]

    def state_begin():
        def pack_state(p):
            parts = []
            for s in (2 * p, 2 * p + 1):
                kept = table[NEW_KEPT, s].astype(F32)
                place = table[NEW_OLD, s]
                both = mv_in[place, core].astype(F32) * kept
                parts.append((core_rows(w1_in[place]) * kept, both[:ROWS], both[ROWS:]))
            for i in range(3):
                state[t, i * half_dev + p] = stack(parts[0][i], parts[1][i])

        loop_by(4, half_dev, pack_state)
        ag_start(*ag_state)

    def product(k):
        both = w_all[:, k].astype(F32)
        for i in range(2):
            n = 2 * k + i
            w = both[:, i * ROWS : (i + 1) * ROWS].reshape(BLOCK, BLOCK).astype(BF16)
            p = jnp.dot(hid_b[table[ROW_ROW, n]], w, preferred_element_type=F32) * scale
            prod[n] = p.reshape(2, half, BLOCK)

    def gather_part(h):
        def column(c):
            total = prod[table[CELL, c], h]
            for r in range(1, row_share):
                total += prod[table[CELL + r, c], h]
            part[h, c] = total.astype(BF16)

        loop_by(8, cols, column)

    swap = remote(part.at[1 - core], part_sib, fwd_send.at[4], fwd_recv.at[4], sibling)

    def part_begin():
        loop_by(8, pairs, product)
        gather_part(1 - core)
        swap.start()

    def term(zz):
        at = pl.ds((zz % chips) * chunk, chunk)
        return part[core, at].astype(F32) + part_sib[at].astype(F32)

    def rs_hop(way, distance):
        step = JUMP if distance == JUMP else 1
        return remote(
            rs_out.at[way, distance],
            rs_in.at[way, distance],
            rs_send.at[way, distance],
            rs_recv.at[way, distance],
            along_z(step if way == 0 else chips - step),
        )

    def rs_step(way, distance):
        if distance > reach[way]:
            return
        value = term(z + distance if way == 0 else z + chips - distance)
        if distance not in (JUMP - 1, reach[way]):
            rs_hop(way, distance + 1).wait_recv()
            value += rs_in[way, distance + 1].astype(F32)
        rs_out[way, distance] = value.astype(BF16)
        rs_hop(way, distance).start()

    def rs_round(k):
        for way in range(2):
            if reach[way] - k >= JUMP:
                rs_step(way, reach[way] - k)
        for way in range(2):
            if JUMP - 1 - k >= 1:
                rs_step(way, min(JUMP - 1, reach[way]) - k)

    finish = remote(fin.at[core], fin.at[core], fwd_send.at[5], fwd_recv.at[5], sibling)

    def rs_end():
        value = term(z)
        for way in range(2):
            for distance in (1, JUMP):
                if distance <= reach[way]:
                    rs_hop(way, distance).wait_recv()
                    value += rs_in[way, distance].astype(F32)
        fin[core] = value.astype(BF16)
        finish.start()

    def ga_begin():
        def pack_g(p):
            g_all[t, p] = stack(*[core_rows(g_new[table[NEW_ROW, s]]) for s in (2 * p, 2 * p + 1)])

        loop_by(4, half_dev, pack_g)
        ag_start(*ag_g)

    cot_begin()
    w1_begin()
    lay_mv()
    lay_hid()
    cot_step(1)
    z_wait("w1")
    cot_step(5)
    fwd["w1"].wait_recv()
    w2_begin()
    for distance in (2, 6, 3, 7):
        cot_step(distance)
    z_wait("w2")
    cot_step(4)
    fwd["w2"].wait_recv()
    w_begin()
    cot_step(8)
    z_start("mv")
    ag_pass_on(*ag_w)
    cot_end()
    g_begin()
    g_pass_on()
    z_wait("mv")
    ag_wait(*ag_w)
    part_begin()
    gather_part(core)
    gz_begin()
    fwd["mv"].wait_recv()
    state_begin()
    swap.wait_recv()
    rs_round(0)
    ag_pass_on(*ag_state)
    rs_round(1)
    z_wait("g")
    rs_round(2)
    fwd["g"].wait_recv()
    ga_begin()
    rs_round(3)
    ag_pass_on(*ag_g)
    rs_end()
    ag_wait(*ag_state)
    ag_wait(*ag_g)
    finish.wait_recv()

    cot_aside(0, 0).wait_send()
    for way in range(2):
        for distance in range(1, reach[way] + 1):
            cot_hop(way, distance).wait_send()
            cot_aside(way, distance).wait_send()
            rs_hop(way, distance).wait_send()
    for name in z_all:
        loop(1, chips, lambda d: z_copy(*z_all[name], d).wait_send())
        fwd[name].wait_send()
    for gather in (ag_w, ag_state, ag_g):
        ag_sent(*gather)
    g_each(lambda copy: copy.wait_send())
    for h in range(2):
        loop(1, side, lambda e: g_second(h, e).wait_send())
    swap.wait_send()
    finish.wait_send()


def finish_kernel(step_pairs, y, g_all, state, out_y, out_w, out_m, out_v, turned):
    half_dev = g_all.shape[1]
    step = pl.program_id(0)

    @pl.when(step == 0)
    def _():
        for j in range(y.shape[1]):
            block = jnp.concatenate([y[0, j], y[1, j]], 0).astype(F32)
            turned[j * BLOCK : (j + 1) * BLOCK, :] = block.T
        width = out_y.shape[0]
        at = pl.ds(pl.multiple_of((lax.axis_index("own") % 2) * width, BLOCK // 2), width)
        out_y[...] = turned[at, :].astype(BF16)

    for j in range(step_pairs):
        p = step * step_pairs + j
        g, w, m, v = [
            ref[:, i].astype(F32)
            for ref, i in ((g_all, p), (state, p), (state, half_dev + p), (state, 2 * half_dev + p))
        ]
        for result, value in zip((out_w, out_m, out_v), adam_update(w, m, v, g)):
            for i in range(2):
                part_rows = value[:, i * ROWS : (i + 1) * ROWS]
                result[2 * j + i] = part_rows.reshape(BLOCK, BLOCK).astype(BF16)


def local(hidden, grad_out, old_weight, old_first, old_second, old_blocks, new_blocks, new_owner):
    owners, toks = lax.axis_size("own"), lax.axis_size("tok")
    chips = owners // 2
    per_dev, block = old_weight.shape[0], old_weight.shape[1]
    total = new_owner.shape[0]
    tokens = hidden.shape[0]
    row_share = hidden.shape[1] // block
    width = grad_out.shape[1] * owners
    cols = width // block
    chunk = cols // chips
    half = block // 2
    scale = (total * block * block / width) ** (-0.5)

    vmem = pl.BlockSpec(memory_space=pltpu.VMEM)
    hbm = pl.BlockSpec(memory_space=pltpu.HBM)
    mine = jax.ShapeDtypeStruct((per_dev, 16, block), BF16)
    table, *locs = pl.pallas_call(
        functools.partial(table_kernel, owners, per_dev, row_share, cols),
        out_shape=(jax.ShapeDtypeStruct((TABLE_ROWS, 128), jnp.int32), mine, mine, mine),
        in_specs=[vmem, vmem, vmem, hbm, hbm, hbm],
        out_specs=(vmem,) * 4,
        scratch_shapes=[pltpu.SemaphoreType.DMA((3,))],
        compiler_params=pltpu.CompilerParams(vmem_limit_bytes=TABLE_VMEM * 2**20),
        name="block_table",
    )(new_owner, old_blocks.T, new_blocks.T, old_weight, old_first, old_second)

    dma = pltpu.SemaphoreType.DMA
    ring = chips // 2
    piece = (chunk, half, block)
    y, g_all, state = pl.pallas_call(
        functools.partial(step_kernel, scale),
        out_shape=(
            jax.ShapeDtypeStruct((2,) + piece, BF16),
            jax.ShapeDtypeStruct((toks, per_dev // 2, 16, block), BF16),
            jax.ShapeDtypeStruct((toks, 3 * per_dev // 2, 16, block), BF16),
        ),
        in_specs=[pl.BlockSpec(memory_space=pltpu.SMEM)] + [vmem] * 5,
        out_specs=(vmem,) * 3,
        scratch_shapes=[
            pltpu.VMEM((chips, 16, block), BF16),
            pltpu.VMEM((owners, 16, block), BF16),
            pltpu.VMEM((chips, 16, block), BF16),
            pltpu.VMEM((owners, 16, block), BF16),
            pltpu.VMEM((owners, 16, block), BF16),
            pltpu.VMEM((owners, 2, 16, block), BF16),
            pltpu.VMEM((2 * cols, half, tokens), BF16),
            pltpu.VMEM((row_share, tokens, block), BF16),
            pltpu.VMEM((row_share, block, tokens), BF16),
            pltpu.VMEM((toks, chips, 16, block), BF16),
            pltpu.VMEM((2, 4, 4, chips // 2, 16, block), BF16),
            pltpu.VMEM((2, 4, chips // 2, 16, block), BF16),
            pltpu.VMEM((2, 4, chips // 2, 16, block), BF16),
            pltpu.VMEM((chips, 16, block), BF16),
            pltpu.VMEM((owners, 16, block), BF16),
            pltpu.VMEM((toks, chips, 16, block), BF16),
            pltpu.VMEM((owners + 1, 2, half, block), F32),
            pltpu.VMEM((2, cols, half, block), BF16),
            pltpu.VMEM((cols, half, block), BF16),
            pltpu.VMEM((2, ring + 1) + piece, BF16),
            pltpu.VMEM((2, ring + 1) + piece, BF16),
            dma((2, ring + 1)),
            dma((2, ring + 1)),
            dma((2, ring + 1)),
            dma((2, ring + 1)),
            dma((4, chips)),
            dma((4, chips)),
            dma((6,)),
            dma((6,)),
            dma((4, 2, 5, 4)),
            dma((4, 2, 5, 4)),
            dma((2, ring + 1)),
            dma((2, ring + 1)),
        ],
        compiler_params=pltpu.CompilerParams(
            collective_id=0, has_side_effects=True, vmem_limit_bytes=STEP_VMEM * 2**20
        ),
        name="projection_step",
    )(table, grad_out.T, hidden, *locs)

    step_pairs = 4
    state_spec = pl.BlockSpec((2 * step_pairs, block, block), lambda i: (i, 0, 0))
    state_shape = jax.ShapeDtypeStruct(old_weight.shape, BF16)
    out, *new_state = pl.pallas_call(
        functools.partial(finish_kernel, step_pairs),
        grid=(per_dev // (2 * step_pairs),),
        out_shape=(jax.ShapeDtypeStruct((grad_out.shape[1], tokens), BF16),) + (state_shape,) * 3,
        in_specs=[vmem, vmem, vmem],
        out_specs=(pl.BlockSpec((grad_out.shape[1], tokens), lambda i: (0, 0)),) + (state_spec,) * 3,
        scratch_shapes=[pltpu.VMEM((chunk * block, tokens), F32)],
        compiler_params=pltpu.CompilerParams(vmem_limit_bytes=16 * 2**20),
        name="adam",
    )(y, g_all, state)
    return (out.T, *new_state)


def solution(mesh):
    state = P("own", None, None)
    in_specs = (P("tok", "own"), P("tok", "own"), state, state, state, P(), P(), P())
    out_specs = (P("tok", "own"), state, state, state)
    return jax.shard_map(local, mesh=mesh, in_specs=in_specs, out_specs=out_specs, check_vma=False)
```

```python
import functools

import jax
import jax.numpy as jnp
from jax import lax
from jax.experimental import pallas as pl
from jax.experimental.pallas import tpu as pltpu
from jax.sharding import PartitionSpec as P

MESH = pl.DeviceIdType.MESH

beta_one = 0.9
beta_two = 0.95
rate = 0.1
epsilon = 0.1
fix_one = 1.0 - 0.9**10
fix_two = 1.0 - 0.95**10

BLOCK = 128
ROWS = 8
F32 = jnp.float32
BF16 = jnp.bfloat16


SEND_SLOT = 0
HOP_OLD, HOP_KEPT = 1, 2
ROW_ROW, ROW_COL = 3, 4
NEW_OLD, NEW_ROW, NEW_KEPT = 5, 6, 7
CELL = 8
TABLE_ROWS = 16


def table_kernel(owners, per_dev, row_share, cols, owner_hbm, old_hbm, new_hbm, *refs):
    olds, table_ref, mine_refs, (owner_ref, old_ref, new_ref, sem) = refs[:3], refs[3], refs[4:7], refs[7:]
    rows = pl.ds((lax.axis_index("tok") // 2) * 16, 16)
    copies = [
        pltpu.make_async_copy(old.at[:, rows, :], ref, sem.at[i]) for i, (old, ref) in enumerate(zip(olds, mine_refs))
    ]
    lists = [
        pltpu.make_async_copy(src, ref, sem.at[3 + i])
        for i, (src, ref) in enumerate(((owner_hbm, owner_ref), (old_hbm, old_ref), (new_hbm, new_ref)))
    ]
    for copy in lists + copies:
        copy.start()
    for copy in lists:
        copy.wait()
    me = lax.axis_index("own")
    total = owner_ref.shape[0]
    shape = (cols, total)

    def spread(row):
        return jnp.broadcast_to(row, shape)

    owner = spread(owner_ref[...].reshape(1, total))
    new_row, new_col = spread(new_ref[0:1, :]), spread(new_ref[1:2, :])
    same = (old_ref[0:1, :] == new_ref[0:1, :]) & (old_ref[1:2, :] == new_ref[1:2, :])
    kept = spread(same.astype(jnp.int32))
    slot = lax.broadcasted_iota(jnp.int32, shape, 0)
    index = lax.broadcasted_iota(jnp.int32, shape, 1)
    row_in = new_row - me * row_share
    row_mine = (row_in >= 0) & (row_in < row_share)
    zero = jnp.zeros(shape, jnp.int32)
    lane = lax.broadcasted_iota(jnp.int32, (cols, 128), 1)
    columns = []

    def pick(where, value):
        return jnp.sum(jnp.where(where, value, zero), axis=1, keepdims=True)

    def put(row, value):
        columns.append((row, value))

    def place(value, share):
        own = jnp.zeros_like(value)
        for i in range(1, owners):
            own += (value >= i * share).astype(jnp.int32)
        return (own & 1) * (owners // 2) + (own >> 1)

    local = index - me * per_dev
    put(SEND_SLOT, pick((owner == slot) & (local >= 0) & (local < per_dev), local))

    mine = owner == me
    row_at = new_row - slot * row_share
    hop = pick(mine & (row_at >= 0) & (row_at < row_share), index * 2 + kept)
    put(HOP_OLD, place(hop >> 1, per_dev))
    put(HOP_KEPT, hop & 1)

    at_row = pick((owner == slot) & row_mine, new_col * 256 + row_in)
    put(ROW_COL, at_row >> 8)
    put(ROW_ROW, at_row & 255)

    down = lax.broadcasted_iota(jnp.int32, (total, total), 0)
    across = lax.broadcasted_iota(jnp.int32, (total, total), 1)
    earlier = jnp.where(down < across, 1.0, 0.0).astype(BF16)
    mine_once = jnp.where(mine[:16], 1.0, 0.0).astype(BF16)
    rank = jnp.dot(mine_once, earlier, preferred_element_type=F32)[0:1, :].astype(jnp.int32)
    at_new = pick(mine & (spread(rank) == slot), (index * 2 + kept) * 256 + new_row)
    put(NEW_OLD, place(at_new >> 9, per_dev))
    put(NEW_ROW, place(at_new & 255, row_share))
    put(NEW_KEPT, (at_new >> 8) & 1)

    for r in range(row_share):
        put(CELL + r, owners + pick((row_in == r) & (new_col == slot), owner - owners))

    turned = jnp.zeros((cols, 128), F32)
    for row, value in columns:
        turned = jnp.where(lane == row, value.astype(F32), turned)
    turned = jnp.concatenate([turned, jnp.zeros((128 - cols, 128), F32)], 0).T
    table_ref[...] = turned[:TABLE_ROWS].astype(jnp.int32)
    for copy in copies:
        copy.wait()


def adam_update(weight, first, second, grad):
    moment = beta_one * first + (1.0 - beta_one) * grad
    square = beta_two * second + (1.0 - beta_two) * grad * grad
    change = (rate / fix_one) * moment / (jnp.sqrt(square * (1.0 / fix_two)) + epsilon)
    return weight - change, moment, square


TABLE_VMEM = 53
STEP_VMEM = 48

JUMP = 5


def step_kernel(
    scale,
    table,
    cot,
    hid,
    loc_w,
    loc_m,
    loc_v,
    fin,
    g_all,
    state,
    w1_out,
    w1_in,
    w2_out,
    w2_in,
    mv_out,
    mv_in,
    cot_all,
    hid_b,
    hid_t,
    g_out,
    g_one,
    g_mid,
    g_two,
    g_sum,
    g_new,
    w_all,
    prod,
    part,
    part_sib,
    rs_out,
    rs_in,
    cot_send,
    cot_recv,
    sib_send,
    sib_recv,
    z_send,
    z_recv,
    fwd_send,
    fwd_recv,
    xy_send,
    xy_recv,
    rs_send,
    rs_recv,
):
    toks, owners = lax.axis_size("tok"), lax.axis_size("own")
    side = 4
    chips = owners // 2
    t, o = lax.axis_index("tok"), lax.axis_index("own")
    z, core = o // 2, o % 2
    y, x = t // side, t % side
    sibling = {"tok": t, "own": z * 2 + 1 - core}
    per_dev = loc_w.shape[0]
    half_dev = per_dev // 2
    row_share = hid_t.shape[0]
    cols = part.shape[1]
    units = cot.shape[0] // (BLOCK // 2)
    chunk = cols // chips
    half = BLOCK // 2
    pairs = owners // 2
    reach = (chips // 2, chips - 1 - chips // 2)

    def remote(src, dst, send, recv, device):
        return pltpu.make_async_remote_copy(
            src_ref=src, dst_ref=dst, send_sem=send, recv_sem=recv, device_id=device, device_id_type=MESH
        )

    def along_z(d):
        return {"tok": t, "own": ((z + d) % chips) * 2 + core}

    def tok_at(dy, dx):
        return ((y + dy) % side) * side + (x + dx) % side

    def across(dy, dx):
        return {"tok": tok_at(dy, dx), "own": o}

    def loop(first, last, body):
        def step(i, carry):
            body(i)
            return carry

        lax.fori_loop(first, last, step, 0)

    loc = (loc_w, loc_m, loc_v)

    def loop_by(n, last, body):
        def several(i):
            for j in range(n):
                body(i * n + j)

        loop(0, last // n, several)

    barrier = pltpu.get_barrier_semaphore()

    def greet(device):
        pl.semaphore_signal(barrier, inc=1, device_id=device, device_id_type=MESH)

    greet(sibling)
    loop(1, chips, lambda d: greet(along_z(d)))
    loop(1, side, lambda d: greet(across(0, d)))
    loop(1, side, lambda d: greet(across(d, 0)))

    def is_one(bit):
        return (jnp.zeros((ROWS, BLOCK), jnp.int32) + bit) == 1

    odd_rows, second_core = is_one(t % 2), is_one(core)

    def own_rows(i, k):
        both = loc[i][k].astype(F32)
        return jnp.where(odd_rows, both[ROWS:], both[:ROWS])

    def core_rows(tile):
        both = tile.astype(F32)
        return jnp.where(second_core, both[ROWS:], both[:ROWS])

    def stack(a, b):
        return jnp.concatenate([a, b], 0).astype(BF16)

    for i in range(units):
        cot_all[o * units + i] = cot[i * half : (i + 1) * half, :]

    def pack_w1(k):
        w1_out[k] = stack(own_rows(0, table[SEND_SLOT, 2 * k]), own_rows(0, table[SEND_SLOT, 2 * k + 1]))

    loop_by(4, chips, pack_w1)
    pl.semaphore_wait(barrier, chips - 1 + 1 + 2 * (side - 1))

    def cot_at(way, distance):
        zz = z + chips - distance if way == 0 else z + distance
        own = (zz % chips) * 2 + core
        return cot_all.at[pl.ds(own * units, units)]

    def cot_hop(way, distance):
        step = distance if distance in (1, JUMP) else 1
        ref = cot_at(way, distance - step)
        return remote(
            ref,
            ref,
            cot_send.at[way, distance],
            cot_recv.at[way, distance],
            along_z(step if way == 0 else chips - step),
        )

    def cot_aside(way, distance):
        ref = cot_at(way, distance)
        return remote(ref, ref, sib_send.at[way, distance], sib_recv.at[way, distance], sibling)

    def cot_step(distance):
        for way in range(2):
            if distance <= reach[way]:
                cot_hop(way, distance).wait_recv()
                if distance + 1 <= reach[way] and distance + 1 != JUMP:
                    cot_hop(way, distance + 1).start()
                cot_aside(way, distance).start()

    def far_first(i):
        return chips // 2 + ((i + 1) // 2) * (1 - 2 * (i % 2))

    def z_copy(plane, src, dst, d):
        zz = (z + d) % chips
        return remote(
            src(zz),
            dst.at[core * chips + z],
            z_send.at[plane, d],
            z_recv.at[plane, d],
            {"tok": t, "own": zz * 2 + core},
        )

    def forward(plane, ref):
        return remote(ref, ref, fwd_send.at[plane], fwd_recv.at[plane], sibling)

    my_chips = pl.ds(core * chips, chips)
    z_all = {
        "w1": (0, lambda zz: w1_out.at[zz], w1_in),
        "mv": (1, lambda zz: mv_out.at[pl.ds(2 * zz, 2)], mv_in),
        "w2": (2, lambda zz: w2_out.at[zz], w2_in),
        "g": (3, lambda zz: g_sum.at[zz], g_new),
    }
    fwd = {
        "w1": forward(0, w1_in.at[my_chips]),
        "mv": forward(1, mv_in.at[my_chips, 1 - core]),
        "w2": forward(2, w2_in.at[my_chips]),
        "g": forward(3, g_new.at[my_chips]),
    }

    def z_start(name):
        loop(0, chips - 1, lambda i: z_copy(*z_all[name], far_first(i)).start())

    def z_wait(name):
        loop(1, chips, lambda d: z_copy(*z_all[name], d).wait_recv())
        fwd[name].start()

    def xy_one(plane, at, h, d):
        ref = at(h, t)
        to = across(0, d) if h == 0 else across(d, 0)
        return remote(ref, ref, xy_send.at[plane, h, 0, d], xy_recv.at[plane, h, 0, d], to)

    def xy_two(plane, at, h, e, d):
        ref = at(h, tok_at(0, e) if h == 0 else tok_at(e, 0))
        to = across(d, 0) if h == 0 else across(0, d)
        return remote(ref, ref, xy_send.at[plane, h, 1 + e, d], xy_recv.at[plane, h, 1 + e, d], to)

    def ag_start(plane, at):
        for h in range(2):
            loop(1, side, lambda d: xy_one(plane, at, h, d).start())
        for h in range(2):
            loop(1, side, lambda d: xy_two(plane, at, h, 0, d).start())

    def ag_pass_on(plane, at):
        def pass_on(d):
            for h in range(2):
                xy_one(plane, at, h, d).wait_recv()
                loop(1, side, lambda dd: xy_two(plane, at, h, side - d, dd).start())

        loop(1, side, pass_on)

    def ag_each(plane, at, do):
        for h in range(2):
            loop(0, side, lambda e: loop(1, side, lambda d: do(xy_two(plane, at, h, e, d))))

    def ag_wait(plane, at):
        ag_each(plane, at, lambda copy: copy.wait_recv())

    def ag_sent(plane, at):
        for h in range(2):
            loop(1, side, lambda d: xy_one(plane, at, h, d).wait_send())
        ag_each(plane, at, lambda copy: copy.wait_send())

    def halves(ref):
        n = ref.shape[1] // 2
        return lambda h, i: ref.at[i, pl.ds(h * n, n)]

    ag_w, ag_state, ag_g = (0, halves(w_all)), (1, halves(state)), (2, halves(g_all))

    def cot_begin():
        for way in range(2):
            cot_hop(way, 1).start()
        for way in range(2):
            if JUMP <= reach[way]:
                cot_hop(way, JUMP).start()
        cot_aside(0, 0).start()

    def cot_end():
        cot_aside(0, 0).wait_recv()
        for way in range(2):
            for distance in range(1, reach[way] + 1):
                cot_aside(way, distance).wait_recv()

    def w1_begin():
        z_start("w1")
        w1_in[core * chips + z] = w1_out[z]

    def lay_mv():
        def pack_mv(n):
            k = table[SEND_SLOT, n]
            mv_out[n] = stack(own_rows(1, k), own_rows(2, k))

        loop_by(4, owners, pack_mv)
        mv_in[core * chips + z] = mv_out[pl.ds(2 * z, 2)]

    def lay_hid():
        for r in range(row_share):
            block = hid[:, r * BLOCK : (r + 1) * BLOCK]
            hid_b[r] = block
            hid_t[r] = block.astype(F32).T.astype(BF16)
        prod[owners] = jnp.zeros(prod.shape[1:], F32)

    def w2_begin():
        def pack_w2(k):
            parts = []
            for r in (2 * k, 2 * k + 1):
                parts.append(core_rows(w1_in[table[HOP_OLD, r]]) * table[HOP_KEPT, r].astype(F32))
            w2_out[k] = stack(*parts)

        loop_by(4, chips, pack_w2)
        z_start("w2")
        w2_in[core * chips + z] = w2_out[z]

    def grad_pair(k):
        slices = []
        for n in (2 * k, 2 * k + 1):
            at = table[ROW_COL, n] * 2
            cot_t = jnp.concatenate([cot_all[at], cot_all[at + 1]], 0)
            g = lax.dot_general(
                hid_t[table[ROW_ROW, n]], cot_t, (((1,), (1,)), ((), ())), preferred_element_type=F32
            )
            slices.append((g * scale).reshape(toks, ROWS, BLOCK))
        g_out[:, k] = jnp.concatenate(slices, 1).astype(BF16)

    def half_pairs(h):
        return pl.ds(h * (pairs // 2), pairs // 2)

    def g_first(h, e, d):
        to = tok_at(e, d) if h == 0 else tok_at(d, e)
        return remote(
            g_out.at[to, half_pairs(h)],
            g_one.at[h, d, e],
            xy_send.at[3, h, 1 + e, d],
            xy_recv.at[3, h, 1 + e, d],
            across(0, d) if h == 0 else across(d, 0),
        )

    def g_second(h, e):
        return remote(
            g_mid.at[h, e],
            g_two.at[h, e],
            xy_send.at[3, h, 0, e],
            xy_recv.at[3, h, 0, e],
            across(e, 0) if h == 0 else across(0, e),
        )

    def g_each(do):
        for h in range(2):
            loop(1, side, lambda e: loop(1, side, lambda d: do(g_first(h, e, d))))
        for h in range(2):
            loop(1, side, lambda d: do(g_first(h, 0, d)))

    def g_begin():
        loop_by(8, pairs, grad_pair)
        g_each(lambda copy: copy.start())

    def w_begin():
        def pack_w(k):
            w_all[t, k] = stack(core_rows(w2_in[k]), core_rows(w2_in[chips + k]))

        loop_by(4, pairs, pack_w)
        ag_start(*ag_w)

    def g_middle(e):
        for h in range(2):
            loop(1, side, lambda d: g_first(h, e, d).wait_recv())
            own = g_out[tok_at(e, 0) if h == 0 else tok_at(0, e), half_pairs(h)].astype(F32)
            others = [g_one[h, d, e].astype(F32) for d in range(1, side)]
            g_mid[h, e] = (own + others[0] + others[1] + others[2]).astype(BF16)

    def g_on(e):
        g_middle(e)
        for h in range(2):
            g_second(h, e).start()

    def g_pass_on():
        loop(1, side, g_on)

    def gz_begin():
        g_middle(0)
        for h in range(2):
            loop(1, side, lambda e: g_second(h, e).wait_recv())
            total = g_mid[h, 0].astype(F32)
            for e in range(1, side):
                total += g_two[h, e].astype(F32)
            g_sum[half_pairs(h)] = total.astype(BF16)
        z_start("g")
        g_new[core * chips + z] = g_sum[z]

    def state_begin():
        def pack_state(p):
            parts = []
            for s in (2 * p, 2 * p + 1):
                kept = table[NEW_KEPT, s].astype(F32)
                place = table[NEW_OLD, s]
                both = mv_in[place, core].astype(F32) * kept
                parts.append((core_rows(w1_in[place]) * kept, both[:ROWS], both[ROWS:]))
            for i in range(3):
                state[t, i * half_dev + p] = stack(parts[0][i], parts[1][i])

        loop_by(4, half_dev, pack_state)
        ag_start(*ag_state)

    def product(k):
        both = w_all[:, k].astype(F32)
        for i in range(2):
            n = 2 * k + i
            w = both[:, i * ROWS : (i + 1) * ROWS].reshape(BLOCK, BLOCK).astype(BF16)
            p = jnp.dot(hid_b[table[ROW_ROW, n]], w, preferred_element_type=F32) * scale
            prod[n] = p.reshape(2, half, BLOCK)

    def gather_part(h):
        def column(c):
            total = prod[table[CELL, c], h]
            for r in range(1, row_share):
                total += prod[table[CELL + r, c], h]
            part[h, c] = total.astype(BF16)

        loop_by(8, cols, column)

    swap = remote(part.at[1 - core], part_sib, fwd_send.at[4], fwd_recv.at[4], sibling)

    def part_begin():
        loop_by(8, pairs, product)
        gather_part(1 - core)
        swap.start()

    def term(zz):
        at = pl.ds((zz % chips) * chunk, chunk)
        return part[core, at].astype(F32) + part_sib[at].astype(F32)

    def rs_hop(way, distance):
        step = JUMP if distance == JUMP else 1
        return remote(
            rs_out.at[way, distance],
            rs_in.at[way, distance],
            rs_send.at[way, distance],
            rs_recv.at[way, distance],
            along_z(step if way == 0 else chips - step),
        )

    def rs_step(way, distance):
        if distance > reach[way]:
            return
        value = term(z + distance if way == 0 else z + chips - distance)
        if distance not in (JUMP - 1, reach[way]):
            rs_hop(way, distance + 1).wait_recv()
            value += rs_in[way, distance + 1].astype(F32)
        rs_out[way, distance] = value.astype(BF16)
        rs_hop(way, distance).start()

    def rs_round(k):
        for way in range(2):
            if reach[way] - k >= JUMP:
                rs_step(way, reach[way] - k)
        for way in range(2):
            if JUMP - 1 - k >= 1:
                rs_step(way, min(JUMP - 1, reach[way]) - k)

    finish = remote(fin.at[core], fin.at[core], fwd_send.at[5], fwd_recv.at[5], sibling)

    def rs_end():
        value = term(z)
        for way in range(2):
            for distance in (1, JUMP):
                if distance <= reach[way]:
                    rs_hop(way, distance).wait_recv()
                    value += rs_in[way, distance].astype(F32)
        fin[core] = value.astype(BF16)
        finish.start()

    def ga_begin():
        def pack_g(p):
            g_all[t, p] = stack(*[core_rows(g_new[table[NEW_ROW, s]]) for s in (2 * p, 2 * p + 1)])

        loop_by(4, half_dev, pack_g)
        ag_start(*ag_g)

    cot_begin()
    w1_begin()
    lay_mv()
    lay_hid()
    cot_step(1)
    z_wait("w1")
    cot_step(5)
    fwd["w1"].wait_recv()
    w2_begin()
    for distance in (2, 6, 3, 7):
        cot_step(distance)
    z_wait("w2")
    cot_step(4)
    fwd["w2"].wait_recv()
    w_begin()
    cot_step(8)
    z_start("mv")
    ag_pass_on(*ag_w)
    cot_end()
    g_begin()
    g_pass_on()
    z_wait("mv")
    ag_wait(*ag_w)
    part_begin()
    fwd["mv"].wait_recv()
    state_begin()
    gather_part(core)
    gz_begin()
    swap.wait_recv()
    rs_round(0)
    ag_pass_on(*ag_state)
    rs_round(1)
    z_wait("g")
    rs_round(2)
    fwd["g"].wait_recv()
    ga_begin()
    rs_round(3)
    ag_pass_on(*ag_g)
    rs_end()
    ag_wait(*ag_state)
    ag_wait(*ag_g)
    finish.wait_recv()

    cot_aside(0, 0).wait_send()
    for way in range(2):
        for distance in range(1, reach[way] + 1):
            cot_hop(way, distance).wait_send()
            cot_aside(way, distance).wait_send()
            rs_hop(way, distance).wait_send()
    for name in z_all:
        loop(1, chips, lambda d: z_copy(*z_all[name], d).wait_send())
        fwd[name].wait_send()
    for gather in (ag_w, ag_state, ag_g):
        ag_sent(*gather)
    g_each(lambda copy: copy.wait_send())
    for h in range(2):
        loop(1, side, lambda e: g_second(h, e).wait_send())
    swap.wait_send()
    finish.wait_send()


def finish_kernel(step_pairs, y, g_all, state, out_y, out_w, out_m, out_v, turned):
    half_dev = g_all.shape[1]
    step = pl.program_id(0)

    @pl.when(step == 0)
    def _():
        for j in range(y.shape[1]):
            block = jnp.concatenate([y[0, j], y[1, j]], 0).astype(F32)
            turned[j * BLOCK : (j + 1) * BLOCK, :] = block.T
        width = out_y.shape[0]
        at = pl.ds(pl.multiple_of((lax.axis_index("own") % 2) * width, BLOCK // 2), width)
        out_y[...] = turned[at, :].astype(BF16)

    for j in range(step_pairs):
        p = step * step_pairs + j
        g, w, m, v = [
            ref[:, i].astype(F32)
            for ref, i in ((g_all, p), (state, p), (state, half_dev + p), (state, 2 * half_dev + p))
        ]
        for result, value in zip((out_w, out_m, out_v), adam_update(w, m, v, g)):
            for i in range(2):
                part_rows = value[:, i * ROWS : (i + 1) * ROWS]
                result[2 * j + i] = part_rows.reshape(BLOCK, BLOCK).astype(BF16)


def local(hidden, grad_out, old_weight, old_first, old_second, old_blocks, new_blocks, new_owner):
    owners, toks = lax.axis_size("own"), lax.axis_size("tok")
    chips = owners // 2
    per_dev, block = old_weight.shape[0], old_weight.shape[1]
    total = new_owner.shape[0]
    tokens = hidden.shape[0]
    row_share = hidden.shape[1] // block
    width = grad_out.shape[1] * owners
    cols = width // block
    chunk = cols // chips
    half = block // 2
    scale = (total * block * block / width) ** (-0.5)

    vmem = pl.BlockSpec(memory_space=pltpu.VMEM)
    hbm = pl.BlockSpec(memory_space=pltpu.HBM)
    mine = jax.ShapeDtypeStruct((per_dev, 16, block), BF16)
    table, *locs = pl.pallas_call(
        functools.partial(table_kernel, owners, per_dev, row_share, cols),
        out_shape=(jax.ShapeDtypeStruct((TABLE_ROWS, 128), jnp.int32), mine, mine, mine),
        in_specs=[hbm] * 6,
        out_specs=(vmem,) * 4,
        scratch_shapes=[
            pltpu.VMEM((total,), jnp.int32),
            pltpu.VMEM((2, total), jnp.int32),
            pltpu.VMEM((2, total), jnp.int32),
            pltpu.SemaphoreType.DMA((6,)),
        ],
        compiler_params=pltpu.CompilerParams(vmem_limit_bytes=TABLE_VMEM * 2**20),
        name="block_table",
    )(new_owner, old_blocks.T, new_blocks.T, old_weight, old_first, old_second)

    dma = pltpu.SemaphoreType.DMA
    ring = chips // 2
    piece = (chunk, half, block)
    y, g_all, state = pl.pallas_call(
        functools.partial(step_kernel, scale),
        out_shape=(
            jax.ShapeDtypeStruct((2,) + piece, BF16),
            jax.ShapeDtypeStruct((toks, per_dev // 2, 16, block), BF16),
            jax.ShapeDtypeStruct((toks, 3 * per_dev // 2, 16, block), BF16),
        ),
        in_specs=[pl.BlockSpec(memory_space=pltpu.SMEM)] + [vmem] * 5,
        out_specs=(vmem,) * 3,
        scratch_shapes=[
            pltpu.VMEM((chips, 16, block), BF16),
            pltpu.VMEM((owners, 16, block), BF16),
            pltpu.VMEM((chips, 16, block), BF16),
            pltpu.VMEM((owners, 16, block), BF16),
            pltpu.VMEM((owners, 16, block), BF16),
            pltpu.VMEM((owners, 2, 16, block), BF16),
            pltpu.VMEM((2 * cols, half, tokens), BF16),
            pltpu.VMEM((row_share, tokens, block), BF16),
            pltpu.VMEM((row_share, block, tokens), BF16),
            pltpu.VMEM((toks, chips, 16, block), BF16),
            pltpu.VMEM((2, 4, 4, chips // 2, 16, block), BF16),
            pltpu.VMEM((2, 4, chips // 2, 16, block), BF16),
            pltpu.VMEM((2, 4, chips // 2, 16, block), BF16),
            pltpu.VMEM((chips, 16, block), BF16),
            pltpu.VMEM((owners, 16, block), BF16),
            pltpu.VMEM((toks, chips, 16, block), BF16),
            pltpu.VMEM((owners + 1, 2, half, block), F32),
            pltpu.VMEM((2, cols, half, block), BF16),
            pltpu.VMEM((cols, half, block), BF16),
            pltpu.VMEM((2, ring + 1) + piece, BF16),
            pltpu.VMEM((2, ring + 1) + piece, BF16),
            dma((2, ring + 1)),
            dma((2, ring + 1)),
            dma((2, ring + 1)),
            dma((2, ring + 1)),
            dma((4, chips)),
            dma((4, chips)),
            dma((6,)),
            dma((6,)),
            dma((4, 2, 5, 4)),
            dma((4, 2, 5, 4)),
            dma((2, ring + 1)),
            dma((2, ring + 1)),
        ],
        compiler_params=pltpu.CompilerParams(
            collective_id=0, has_side_effects=True, vmem_limit_bytes=STEP_VMEM * 2**20
        ),
        name="projection_step",
    )(table, grad_out.T, hidden, *locs)

    step_pairs = 6
    state_spec = pl.BlockSpec((2 * step_pairs, block, block), lambda i: (i, 0, 0))
    state_shape = jax.ShapeDtypeStruct(old_weight.shape, BF16)
    out, *new_state = pl.pallas_call(
        functools.partial(finish_kernel, step_pairs),
        grid=(per_dev // (2 * step_pairs),),
        out_shape=(jax.ShapeDtypeStruct((grad_out.shape[1], tokens), BF16),) + (state_shape,) * 3,
        in_specs=[vmem, vmem, vmem],
        out_specs=(pl.BlockSpec((grad_out.shape[1], tokens), lambda i: (0, 0)),) + (state_spec,) * 3,
        scratch_shapes=[pltpu.VMEM((chunk * block, tokens), F32)],
        compiler_params=pltpu.CompilerParams(vmem_limit_bytes=16 * 2**20),
        name="adam",
    )(y, g_all, state)
    return (out.T, *new_state)


def solution(mesh):
    state = P("own", None, None)
    in_specs = (P("tok", "own"), P("tok", "own"), state, state, state, P(), P(), P())
    out_specs = (P("tok", "own"), state, state, state)
    return jax.shard_map(local, mesh=mesh, in_specs=in_specs, out_specs=out_specs, check_vma=False)
```

```python
import functools

import jax
import jax.numpy as jnp
from jax import lax
from jax.experimental import pallas as pl
from jax.experimental.pallas import tpu as pltpu
from jax.sharding import PartitionSpec as P

MESH = pl.DeviceIdType.MESH

beta_one = 0.9
beta_two = 0.95
rate = 0.1
epsilon = 0.1
fix_one = 1.0 - 0.9**10
fix_two = 1.0 - 0.95**10

BLOCK = 128
ROWS = 8
F32 = jnp.float32
BF16 = jnp.bfloat16


SEND_SLOT = 0
HOP_OLD, HOP_KEPT = 1, 2
ROW_ROW, ROW_COL = 3, 4
NEW_OLD, NEW_ROW, NEW_KEPT = 5, 6, 7
CELL = 8
TABLE_ROWS = 16


def table_kernel(owners, per_dev, row_share, cols, owner_hbm, old_hbm, new_hbm, *refs):
    olds, table_ref, mine_refs, (owner_ref, old_ref, new_ref, sem) = refs[:3], refs[3], refs[4:7], refs[7:]
    rows = pl.ds((lax.axis_index("tok") // 2) * 16, 16)
    copies = [
        pltpu.make_async_copy(old.at[:, rows, :], ref, sem.at[i]) for i, (old, ref) in enumerate(zip(olds, mine_refs))
    ]
    lists = [
        pltpu.make_async_copy(src, ref, sem.at[3 + i])
        for i, (src, ref) in enumerate(((owner_hbm, owner_ref), (old_hbm, old_ref), (new_hbm, new_ref)))
    ]
    for copy in lists + copies:
        copy.start()
    for copy in lists:
        copy.wait()
    me = lax.axis_index("own")
    total = owner_ref.shape[0]
    shape = (cols, total)

    def spread(row):
        return jnp.broadcast_to(row, shape)

    owner = spread(owner_ref[...].reshape(1, total))
    new_row, new_col = spread(new_ref[0:1, :]), spread(new_ref[1:2, :])
    same = (old_ref[0:1, :] == new_ref[0:1, :]) & (old_ref[1:2, :] == new_ref[1:2, :])
    kept = spread(same.astype(jnp.int32))
    slot = lax.broadcasted_iota(jnp.int32, shape, 0)
    index = lax.broadcasted_iota(jnp.int32, shape, 1)
    row_in = new_row - me * row_share
    row_mine = (row_in >= 0) & (row_in < row_share)
    zero = jnp.zeros(shape, jnp.int32)
    lane = lax.broadcasted_iota(jnp.int32, (cols, 128), 1)
    columns = []

    def pick(where, value):
        return jnp.sum(jnp.where(where, value, zero), axis=1, keepdims=True)

    def put(row, value):
        columns.append((row, value))

    def place(value, share):
        own = jnp.zeros_like(value)
        for i in range(1, owners):
            own += (value >= i * share).astype(jnp.int32)
        return (own & 1) * (owners // 2) + (own >> 1)

    local = index - me * per_dev
    put(SEND_SLOT, pick((owner == slot) & (local >= 0) & (local < per_dev), local))

    mine = owner == me
    row_at = new_row - slot * row_share
    hop = pick(mine & (row_at >= 0) & (row_at < row_share), index * 2 + kept)
    put(HOP_OLD, place(hop >> 1, per_dev))
    put(HOP_KEPT, hop & 1)

    at_row = pick((owner == slot) & row_mine, new_col * 256 + row_in)
    put(ROW_COL, at_row >> 8)
    put(ROW_ROW, at_row & 255)

    down = lax.broadcasted_iota(jnp.int32, (total, total), 0)
    across = lax.broadcasted_iota(jnp.int32, (total, total), 1)
    earlier = jnp.where(down < across, 1.0, 0.0).astype(BF16)
    mine_once = jnp.where(mine[:16], 1.0, 0.0).astype(BF16)
    rank = jnp.dot(mine_once, earlier, preferred_element_type=F32)[0:1, :].astype(jnp.int32)
    at_new = pick(mine & (spread(rank) == slot), (index * 2 + kept) * 256 + new_row)
    put(NEW_OLD, place(at_new >> 9, per_dev))
    put(NEW_ROW, place(at_new & 255, row_share))
    put(NEW_KEPT, (at_new >> 8) & 1)

    for r in range(row_share):
        put(CELL + r, owners + pick((row_in == r) & (new_col == slot), owner - owners))

    turned = jnp.zeros((cols, 128), F32)
    for row, value in columns:
        turned = jnp.where(lane == row, value.astype(F32), turned)
    turned = jnp.concatenate([turned, jnp.zeros((128 - cols, 128), F32)], 0).T
    table_ref[...] = turned[:TABLE_ROWS].astype(jnp.int32)
    for copy in copies:
        copy.wait()


def adam_update(weight, first, second, grad):
    moment = beta_one * first + (1.0 - beta_one) * grad
    square = beta_two * second + (1.0 - beta_two) * grad * grad
    change = (rate / fix_one) * moment / (jnp.sqrt(square * (1.0 / fix_two)) + epsilon)
    return weight - change, moment, square


TABLE_VMEM = 53
STEP_VMEM = 48

JUMP = 5


def step_kernel(
    scale,
    table,
    cot,
    hid,
    loc_w,
    loc_m,
    loc_v,
    fin,
    g_all,
    state,
    w1_out,
    w1_in,
    w2_out,
    w2_in,
    mv_out,
    mv_in,
    cot_all,
    hid_b,
    hid_t,
    g_out,
    g_one,
    g_mid,
    g_two,
    g_sum,
    g_new,
    w_all,
    prod,
    part,
    part_sib,
    rs_out,
    rs_in,
    cot_send,
    cot_recv,
    sib_send,
    sib_recv,
    z_send,
    z_recv,
    fwd_send,
    fwd_recv,
    xy_send,
    xy_recv,
    rs_send,
    rs_recv,
):
    toks, owners = lax.axis_size("tok"), lax.axis_size("own")
    side = 4
    chips = owners // 2
    t, o = lax.axis_index("tok"), lax.axis_index("own")
    z, core = o // 2, o % 2
    y, x = t // side, t % side
    sibling = {"tok": t, "own": z * 2 + 1 - core}
    per_dev = loc_w.shape[0]
    half_dev = per_dev // 2
    row_share = hid_t.shape[0]
    cols = part.shape[1]
    units = cot.shape[0] // (BLOCK // 2)
    chunk = cols // chips
    half = BLOCK // 2
    pairs = owners // 2
    reach = (chips // 2, chips - 1 - chips // 2)

    def remote(src, dst, send, recv, device):
        return pltpu.make_async_remote_copy(
            src_ref=src, dst_ref=dst, send_sem=send, recv_sem=recv, device_id=device, device_id_type=MESH
        )

    def along_z(d):
        return {"tok": t, "own": ((z + d) % chips) * 2 + core}

    def tok_at(dy, dx):
        return ((y + dy) % side) * side + (x + dx) % side

    def across(dy, dx):
        return {"tok": tok_at(dy, dx), "own": o}

    def loop(first, last, body):
        def step(i, carry):
            body(i)
            return carry

        lax.fori_loop(first, last, step, 0)

    loc = (loc_w, loc_m, loc_v)

    def loop_by(n, last, body):
        def several(i):
            for j in range(n):
                body(i * n + j)

        loop(0, last // n, several)

    barrier = pltpu.get_barrier_semaphore()

    def greet(device):
        pl.semaphore_signal(barrier, inc=1, device_id=device, device_id_type=MESH)

    greet(sibling)
    loop(1, chips, lambda d: greet(along_z(d)))
    loop(1, side, lambda d: greet(across(0, d)))
    loop(1, side, lambda d: greet(across(d, 0)))

    def is_one(bit):
        return (jnp.zeros((ROWS, BLOCK), jnp.int32) + bit) == 1

    odd_rows, second_core = is_one(t % 2), is_one(core)

    def own_rows(i, k):
        both = loc[i][k].astype(F32)
        return jnp.where(odd_rows, both[ROWS:], both[:ROWS])

    def core_rows(tile):
        both = tile.astype(F32)
        return jnp.where(second_core, both[ROWS:], both[:ROWS])

    def stack(a, b):
        return jnp.concatenate([a, b], 0).astype(BF16)

    for i in range(units):
        cot_all[o * units + i] = cot[i * half : (i + 1) * half, :]

    def pack_w1(k):
        w1_out[k] = stack(own_rows(0, table[SEND_SLOT, 2 * k]), own_rows(0, table[SEND_SLOT, 2 * k + 1]))

    loop_by(4, chips, pack_w1)
    pl.semaphore_wait(barrier, chips - 1 + 1 + 2 * (side - 1))

    def cot_at(way, distance):
        zz = z + chips - distance if way == 0 else z + distance
        own = (zz % chips) * 2 + core
        return cot_all.at[pl.ds(own * units, units)]

    def cot_hop(way, distance):
        step = distance if distance in (1, JUMP) else 1
        ref = cot_at(way, distance - step)
        return remote(
            ref,
            ref,
            cot_send.at[way, distance],
            cot_recv.at[way, distance],
            along_z(step if way == 0 else chips - step),
        )

    def cot_aside(way, distance):
        ref = cot_at(way, distance)
        return remote(ref, ref, sib_send.at[way, distance], sib_recv.at[way, distance], sibling)

    def cot_step(distance):
        for way in range(2):
            if distance <= reach[way]:
                cot_hop(way, distance).wait_recv()
                if distance + 1 <= reach[way] and distance + 1 != JUMP:
                    cot_hop(way, distance + 1).start()
                cot_aside(way, distance).start()

    def far_first(i):
        return chips // 2 + ((i + 1) // 2) * (1 - 2 * (i % 2))

    def z_copy(plane, src, dst, d):
        zz = (z + d) % chips
        return remote(
            src(zz),
            dst.at[core * chips + z],
            z_send.at[plane, d],
            z_recv.at[plane, d],
            {"tok": t, "own": zz * 2 + core},
        )

    def forward(plane, ref):
        return remote(ref, ref, fwd_send.at[plane], fwd_recv.at[plane], sibling)

    my_chips = pl.ds(core * chips, chips)
    z_all = {
        "w1": (0, lambda zz: w1_out.at[zz], w1_in),
        "mv": (1, lambda zz: mv_out.at[pl.ds(2 * zz, 2)], mv_in),
        "w2": (2, lambda zz: w2_out.at[zz], w2_in),
        "g": (3, lambda zz: g_sum.at[zz], g_new),
    }
    fwd = {
        "w1": forward(0, w1_in.at[my_chips]),
        "mv": forward(1, mv_in.at[my_chips, 1 - core]),
        "w2": forward(2, w2_in.at[my_chips]),
        "g": forward(3, g_new.at[my_chips]),
    }

    def z_start(name):
        for i in range(chips - 1):
            z_copy(*z_all[name], far_first(i)).start()

    def z_wait(name):
        loop(1, chips, lambda d: z_copy(*z_all[name], d).wait_recv())
        fwd[name].start()

    def xy_one(plane, at, h, d):
        ref = at(h, t)
        to = across(0, d) if h == 0 else across(d, 0)
        return remote(ref, ref, xy_send.at[plane, h, 0, d], xy_recv.at[plane, h, 0, d], to)

    def xy_two(plane, at, h, e, d):
        ref = at(h, tok_at(0, e) if h == 0 else tok_at(e, 0))
        to = across(d, 0) if h == 0 else across(0, d)
        return remote(ref, ref, xy_send.at[plane, h, 1 + e, d], xy_recv.at[plane, h, 1 + e, d], to)

    def ag_start(plane, at):
        for h in range(2):
            for d in range(1, side):
                xy_one(plane, at, h, d).start()
        for h in range(2):
            for d in range(1, side):
                xy_two(plane, at, h, 0, d).start()

    def ag_pass_on(plane, at):
        def pass_on(d):
            for h in range(2):
                xy_one(plane, at, h, d).wait_recv()
                for dd in range(1, side):
                    xy_two(plane, at, h, side - d, dd).start()

        for d in (1, 3, 2):
            pass_on(d)

    def ag_each(plane, at, do):
        for h in range(2):
            loop(0, side, lambda e: loop(1, side, lambda d: do(xy_two(plane, at, h, e, d))))

    def ag_wait(plane, at):
        ag_each(plane, at, lambda copy: copy.wait_recv())

    def ag_sent(plane, at):
        for h in range(2):
            loop(1, side, lambda d: xy_one(plane, at, h, d).wait_send())
        ag_each(plane, at, lambda copy: copy.wait_send())

    def halves(ref):
        n = ref.shape[1] // 2
        return lambda h, i: ref.at[i, pl.ds(h * n, n)]

    ag_w, ag_state, ag_g = (0, halves(w_all)), (1, halves(state)), (2, halves(g_all))

    def cot_begin():
        for way in range(2):
            cot_hop(way, 1).start()
        for way in range(2):
            if JUMP <= reach[way]:
                cot_hop(way, JUMP).start()
        cot_aside(0, 0).start()

    def cot_end():
        cot_aside(0, 0).wait_recv()
        for way in range(2):
            for distance in range(1, reach[way] + 1):
                cot_aside(way, distance).wait_recv()

    def w1_begin():
        z_start("w1")
        w1_in[core * chips + z] = w1_out[z]

    def lay_mv():
        def pack_mv(n):
            k = table[SEND_SLOT, n]
            mv_out[n] = stack(own_rows(1, k), own_rows(2, k))

        loop_by(4, owners, pack_mv)
        mv_in[core * chips + z] = mv_out[pl.ds(2 * z, 2)]

    def lay_hid():
        for r in range(row_share):
            block = hid[:, r * BLOCK : (r + 1) * BLOCK]
            hid_b[r] = block
            hid_t[r] = block.astype(F32).T.astype(BF16)
        prod[owners] = jnp.zeros(prod.shape[1:], F32)

    def w2_begin():
        def pack_w2(k):
            parts = []
            for r in (2 * k, 2 * k + 1):
                parts.append(core_rows(w1_in[table[HOP_OLD, r]]) * table[HOP_KEPT, r].astype(F32))
            w2_out[k] = stack(*parts)

        loop_by(4, chips, pack_w2)
        z_start("w2")
        w2_in[core * chips + z] = w2_out[z]

    def grad_pair(k):
        slices = []
        for n in (2 * k, 2 * k + 1):
            at = table[ROW_COL, n] * 2
            cot_t = jnp.concatenate([cot_all[at], cot_all[at + 1]], 0)
            g = lax.dot_general(
                hid_t[table[ROW_ROW, n]], cot_t, (((1,), (1,)), ((), ())), preferred_element_type=F32
            )
            slices.append((g * scale).reshape(toks, ROWS, BLOCK))
        g_out[:, k] = jnp.concatenate(slices, 1).astype(BF16)

    def half_pairs(h):
        return pl.ds(h * (pairs // 2), pairs // 2)

    def g_first(h, e, d):
        to = tok_at(e, d) if h == 0 else tok_at(d, e)
        return remote(
            g_out.at[to, half_pairs(h)],
            g_one.at[h, d, e],
            xy_send.at[3, h, 1 + e, d],
            xy_recv.at[3, h, 1 + e, d],
            across(0, d) if h == 0 else across(d, 0),
        )

    def g_second(h, e):
        return remote(
            g_mid.at[h, e],
            g_two.at[h, e],
            xy_send.at[3, h, 0, e],
            xy_recv.at[3, h, 0, e],
            across(e, 0) if h == 0 else across(0, e),
        )

    def g_each(do):
        for h in range(2):
            loop(1, side, lambda e: loop(1, side, lambda d: do(g_first(h, e, d))))
        for h in range(2):
            loop(1, side, lambda d: do(g_first(h, 0, d)))

    def g_begin():
        loop_by(8, pairs, grad_pair)
        g_each(lambda copy: copy.start())

    def w_begin():
        def pack_w(k):
            w_all[t, k] = stack(core_rows(w2_in[k]), core_rows(w2_in[chips + k]))

        loop_by(4, pairs, pack_w)
        ag_start(*ag_w)

    def g_middle(e):
        for h in range(2):
            loop(1, side, lambda d: g_first(h, e, d).wait_recv())
            own = g_out[tok_at(e, 0) if h == 0 else tok_at(0, e), half_pairs(h)].astype(F32)
            others = [g_one[h, d, e].astype(F32) for d in range(1, side)]
            g_mid[h, e] = (own + others[0] + others[1] + others[2]).astype(BF16)

    def g_on(e):
        g_middle(e)
        for h in range(2):
            g_second(h, e).start()

    def g_pass_on():
        loop(1, side, g_on)

    def gz_begin():
        g_middle(0)
        for h in range(2):
            loop(1, side, lambda e: g_second(h, e).wait_recv())
            total = g_mid[h, 0].astype(F32)
            for e in range(1, side):
                total += g_two[h, e].astype(F32)
            g_sum[half_pairs(h)] = total.astype(BF16)
        z_start("g")
        g_new[core * chips + z] = g_sum[z]

    def state_begin():
        def pack_state(p):
            parts = []
            for s in (2 * p, 2 * p + 1):
                kept = table[NEW_KEPT, s].astype(F32)
                place = table[NEW_OLD, s]
                both = mv_in[place, core].astype(F32) * kept
                parts.append((core_rows(w1_in[place]) * kept, both[:ROWS], both[ROWS:]))
            for i in range(3):
                state[t, i * half_dev + p] = stack(parts[0][i], parts[1][i])

        loop_by(4, half_dev, pack_state)
        ag_start(*ag_state)

    def product(k):
        both = w_all[:, k].astype(F32)
        for i in range(2):
            n = 2 * k + i
            w = both[:, i * ROWS : (i + 1) * ROWS].reshape(BLOCK, BLOCK).astype(BF16)
            p = jnp.dot(hid_b[table[ROW_ROW, n]], w, preferred_element_type=F32) * scale
            prod[n] = p.reshape(2, half, BLOCK)

    def gather_part(h):
        def column(c):
            total = prod[table[CELL, c], h]
            for r in range(1, row_share):
                total += prod[table[CELL + r, c], h]
            part[h, c] = total.astype(BF16)

        loop_by(8, cols, column)

    swap = remote(part.at[1 - core], part_sib, fwd_send.at[4], fwd_recv.at[4], sibling)

    def part_begin():
        loop_by(8, pairs, product)
        gather_part(1 - core)
        swap.start()

    def term(zz):
        at = pl.ds((zz % chips) * chunk, chunk)
        return part[core, at].astype(F32) + part_sib[at].astype(F32)

    def rs_hop(way, distance):
        step = JUMP if distance == JUMP else 1
        return remote(
            rs_out.at[way, distance],
            rs_in.at[way, distance],
            rs_send.at[way, distance],
            rs_recv.at[way, distance],
            along_z(step if way == 0 else chips - step),
        )

    def rs_step(way, distance):
        if distance > reach[way]:
            return
        value = term(z + distance if way == 0 else z + chips - distance)
        if distance not in (JUMP - 1, reach[way]):
            rs_hop(way, distance + 1).wait_recv()
            value += rs_in[way, distance + 1].astype(F32)
        rs_out[way, distance] = value.astype(BF16)
        rs_hop(way, distance).start()

    def rs_round(k):
        for way in range(2):
            if reach[way] - k >= JUMP:
                rs_step(way, reach[way] - k)
        for way in range(2):
            if JUMP - 1 - k >= 1:
                rs_step(way, min(JUMP - 1, reach[way]) - k)

    finish = remote(fin.at[core], fin.at[core], fwd_send.at[5], fwd_recv.at[5], sibling)

    def rs_end():
        value = term(z)
        for way in range(2):
            for distance in (1, JUMP):
                if distance <= reach[way]:
                    rs_hop(way, distance).wait_recv()
                    value += rs_in[way, distance].astype(F32)
        fin[core] = value.astype(BF16)
        finish.start()

    def ga_begin():
        def pack_g(p):
            g_all[t, p] = stack(*[core_rows(g_new[table[NEW_ROW, s]]) for s in (2 * p, 2 * p + 1)])

        loop_by(4, half_dev, pack_g)
        ag_start(*ag_g)

    cot_begin()
    w1_begin()
    lay_mv()
    lay_hid()
    cot_step(1)
    z_wait("w1")
    cot_step(5)
    fwd["w1"].wait_recv()
    w2_begin()
    for distance in (2, 6, 3, 7):
        cot_step(distance)
    z_wait("w2")
    cot_step(4)
    fwd["w2"].wait_recv()
    w_begin()
    cot_step(8)
    z_start("mv")
    ag_pass_on(*ag_w)
    cot_end()
    g_begin()
    g_pass_on()
    z_wait("mv")
    ag_wait(*ag_w)
    part_begin()
    fwd["mv"].wait_recv()
    state_begin()
    gather_part(core)
    gz_begin()
    swap.wait_recv()
    rs_round(0)
    ag_pass_on(*ag_state)
    rs_round(1)
    z_wait("g")
    rs_round(2)
    fwd["g"].wait_recv()
    ga_begin()
    rs_round(3)
    ag_pass_on(*ag_g)
    rs_end()
    ag_wait(*ag_state)
    ag_wait(*ag_g)
    finish.wait_recv()

    cot_aside(0, 0).wait_send()
    for way in range(2):
        for distance in range(1, reach[way] + 1):
            cot_hop(way, distance).wait_send()
            cot_aside(way, distance).wait_send()
            rs_hop(way, distance).wait_send()
    for name in z_all:
        loop(1, chips, lambda d: z_copy(*z_all[name], d).wait_send())
        fwd[name].wait_send()
    for gather in (ag_w, ag_state, ag_g):
        ag_sent(*gather)
    g_each(lambda copy: copy.wait_send())
    for h in range(2):
        loop(1, side, lambda e: g_second(h, e).wait_send())
    swap.wait_send()
    finish.wait_send()


def finish_kernel(step_pairs, y, g_all, state, out_y, out_w, out_m, out_v, turned):
    half_dev = g_all.shape[1]
    step = pl.program_id(0)

    @pl.when(step == 0)
    def _():
        for j in range(y.shape[1]):
            block = jnp.concatenate([y[0, j], y[1, j]], 0).astype(F32)
            turned[j * BLOCK : (j + 1) * BLOCK, :] = block.T
        width = out_y.shape[0]
        at = pl.ds(pl.multiple_of((lax.axis_index("own") % 2) * width, BLOCK // 2), width)
        out_y[...] = turned[at, :].astype(BF16)

    for j in range(step_pairs):
        p = step * step_pairs + j
        g, w, m, v = [
            ref[:, i].astype(F32)
            for ref, i in ((g_all, p), (state, p), (state, half_dev + p), (state, 2 * half_dev + p))
        ]
        for result, value in zip((out_w, out_m, out_v), adam_update(w, m, v, g)):
            for i in range(2):
                part_rows = value[:, i * ROWS : (i + 1) * ROWS]
                result[2 * j + i] = part_rows.reshape(BLOCK, BLOCK).astype(BF16)


def local(hidden, grad_out, old_weight, old_first, old_second, old_blocks, new_blocks, new_owner):
    owners, toks = lax.axis_size("own"), lax.axis_size("tok")
    chips = owners // 2
    per_dev, block = old_weight.shape[0], old_weight.shape[1]
    total = new_owner.shape[0]
    tokens = hidden.shape[0]
    row_share = hidden.shape[1] // block
    width = grad_out.shape[1] * owners
    cols = width // block
    chunk = cols // chips
    half = block // 2
    scale = (total * block * block / width) ** (-0.5)

    vmem = pl.BlockSpec(memory_space=pltpu.VMEM)
    hbm = pl.BlockSpec(memory_space=pltpu.HBM)
    mine = jax.ShapeDtypeStruct((per_dev, 16, block), BF16)
    table, *locs = pl.pallas_call(
        functools.partial(table_kernel, owners, per_dev, row_share, cols),
        out_shape=(jax.ShapeDtypeStruct((TABLE_ROWS, 128), jnp.int32), mine, mine, mine),
        in_specs=[hbm] * 6,
        out_specs=(vmem,) * 4,
        scratch_shapes=[
            pltpu.VMEM((total,), jnp.int32),
            pltpu.VMEM((2, total), jnp.int32),
            pltpu.VMEM((2, total), jnp.int32),
            pltpu.SemaphoreType.DMA((6,)),
        ],
        compiler_params=pltpu.CompilerParams(vmem_limit_bytes=TABLE_VMEM * 2**20),
        name="block_table",
    )(new_owner, old_blocks.T, new_blocks.T, old_weight, old_first, old_second)

    dma = pltpu.SemaphoreType.DMA
    ring = chips // 2
    piece = (chunk, half, block)
    y, g_all, state = pl.pallas_call(
        functools.partial(step_kernel, scale),
        out_shape=(
            jax.ShapeDtypeStruct((2,) + piece, BF16),
            jax.ShapeDtypeStruct((toks, per_dev // 2, 16, block), BF16),
            jax.ShapeDtypeStruct((toks, 3 * per_dev // 2, 16, block), BF16),
        ),
        in_specs=[pl.BlockSpec(memory_space=pltpu.SMEM)] + [vmem] * 5,
        out_specs=(vmem,) * 3,
        scratch_shapes=[
            pltpu.VMEM((chips, 16, block), BF16),
            pltpu.VMEM((owners, 16, block), BF16),
            pltpu.VMEM((chips, 16, block), BF16),
            pltpu.VMEM((owners, 16, block), BF16),
            pltpu.VMEM((owners, 16, block), BF16),
            pltpu.VMEM((owners, 2, 16, block), BF16),
            pltpu.VMEM((2 * cols, half, tokens), BF16),
            pltpu.VMEM((row_share, tokens, block), BF16),
            pltpu.VMEM((row_share, block, tokens), BF16),
            pltpu.VMEM((toks, chips, 16, block), BF16),
            pltpu.VMEM((2, 4, 4, chips // 2, 16, block), BF16),
            pltpu.VMEM((2, 4, chips // 2, 16, block), BF16),
            pltpu.VMEM((2, 4, chips // 2, 16, block), BF16),
            pltpu.VMEM((chips, 16, block), BF16),
            pltpu.VMEM((owners, 16, block), BF16),
            pltpu.VMEM((toks, chips, 16, block), BF16),
            pltpu.VMEM((owners + 1, 2, half, block), F32),
            pltpu.VMEM((2, cols, half, block), BF16),
            pltpu.VMEM((cols, half, block), BF16),
            pltpu.VMEM((2, ring + 1) + piece, BF16),
            pltpu.VMEM((2, ring + 1) + piece, BF16),
            dma((2, ring + 1)),
            dma((2, ring + 1)),
            dma((2, ring + 1)),
            dma((2, ring + 1)),
            dma((4, chips)),
            dma((4, chips)),
            dma((6,)),
            dma((6,)),
            dma((4, 2, 5, 4)),
            dma((4, 2, 5, 4)),
            dma((2, ring + 1)),
            dma((2, ring + 1)),
        ],
        compiler_params=pltpu.CompilerParams(
            collective_id=0, has_side_effects=True, vmem_limit_bytes=STEP_VMEM * 2**20
        ),
        name="projection_step",
    )(table, grad_out.T, hidden, *locs)

    step_pairs = 6
    state_spec = pl.BlockSpec((2 * step_pairs, block, block), lambda i: (i, 0, 0))
    state_shape = jax.ShapeDtypeStruct(old_weight.shape, BF16)
    out, *new_state = pl.pallas_call(
        functools.partial(finish_kernel, step_pairs),
        grid=(per_dev // (2 * step_pairs),),
        out_shape=(jax.ShapeDtypeStruct((grad_out.shape[1], tokens), BF16),) + (state_shape,) * 3,
        in_specs=[vmem, vmem, vmem],
        out_specs=(pl.BlockSpec((grad_out.shape[1], tokens), lambda i: (0, 0)),) + (state_spec,) * 3,
        scratch_shapes=[pltpu.VMEM((chunk * block, tokens), F32)],
        compiler_params=pltpu.CompilerParams(vmem_limit_bytes=16 * 2**20),
        name="adam",
    )(y, g_all, state)
    return (out.T, *new_state)


def solution(mesh):
    state = P("own", None, None)
    in_specs = (P("tok", "own"), P("tok", "own"), state, state, state, P(), P(), P())
    out_specs = (P("tok", "own"), state, state, state)
    return jax.shard_map(local, mesh=mesh, in_specs=in_specs, out_specs=out_specs, check_vma=False)
```
